128 devices in a mesh: cam: 32 (over y, x, core), row: 4 (over z).
Axes of the slice: x: 4, y: 4, z: 4, core: 2. Of those that a mesh axis runs over, the one named last changes fastest.
Arguments:
- image: bfloat16 [32, 16, 128, 2048], P('cam', None, 'row'), may hold values from -6 to 6
- conv_first: bfloat16 [16, 144], replicated, may hold values from -0.5 to 0.5
- conv_second: bfloat16 [16, 144], replicated, may hold values from -0.5 to 0.5
- conv_uv: bfloat16 [16, 144], replicated, may hold values from -0.5 to 0.5
- send_block: int32 [32, 4, 128, 16], P('cam', 'row'), may hold values from 0 to 511
- send_shift: int32 [32, 4, 128, 16], P('cam', 'row'), may hold values from 0 to 127
- send_weight: int32 [32, 4, 128, 16], P('cam', 'row'), may hold values from 1 to 64
- send_count: int32 [32, 4, 128], P('cam', 'row'), may hold values from 0 to 16, as said below
- recv_tile: int32 [4, 32, 128, 16], P('row', 'cam'), may hold values from 0 to 1023
Outputs:
- texture: bfloat16 [16, 4096, 4096], P(None, 'row', 'cam')
The draws below stay inside these ranges and needn't reach their ends.
Inputs may be any that keep to these rules, and one draw needn't show every extreme that they name: `send_count`: slots of a list at or beyond its count are padding. In every draw one atlas region receives 16 used slots from every strip.
All inputs are finite; a program needn't handle non-finite values.
Results may differ from the reference program's by a relative error of at most 0.0066.
Values may be sent and summed in bfloat16 or wider, within the bound.
A program may use at most 192 MiB of HBM per device.

```python
import jax
import jax.numpy as jnp
from jax import lax

C = 16
W = 2048
H_DEV = 32
TL = 128
CAP = 16
AR_DEV = 1024
CAMS = 32
STRIPS = 4
H = 128
NB = 512
AR = 4096
AC = 4096


def draw_send_count(key, part):
    key_pop = jax.random.fold_in(key, 11)
    key_raw = jax.random.fold_in(key, 12)
    key_full = jax.random.fold_in(key, 13)
    regions = CAMS * STRIPS
    popular = jax.random.randint(key_pop, (regions,), 2, 6)
    raw = jax.random.randint(key_raw, (CAMS, STRIPS, regions), 0, 1 << 20)
    raw = raw % (CAP * popular[None, None, :] // 4 + 1)
    counts = jnp.minimum(raw, CAP)
    full_region = jax.random.randint(key_full, (), 0, regions)
    target = lax.broadcasted_iota(jnp.int32, (CAMS, STRIPS, regions), 2)
    return jnp.where(target == full_region, CAP, counts).astype(jnp.int32)


def plant(drawn, stream_key, smallest, high):
    longest = drawn.shape.index(max(drawn.shape))
    spots = []
    for shift in (0, 1):
        where = [jax.random.randint(jax.random.fold_in(stream_key, axis), (), 0, length) for axis, length in enumerate(drawn.shape)]
        where[longest] = (where[longest] + shift) % drawn.shape[longest]
        spots.append(tuple(where))
    return drawn.at[spots[0]].set(smallest).at[spots[1]].set(high)


def level_of(own_key, extent, shards, smallest, top_value):
    loudness = 1.0
    for axis_at, parts in shards:
        draws = jax.random.uniform(jax.random.fold_in(jax.random.fold_in(own_key, 6), axis_at), (parts,), jnp.float32, smallest / len(shards), top_value / len(shards))
        loudness = loudness * jnp.repeat(jnp.exp(draws), extent[axis_at] // parts).reshape((-1,) + (1,) * (len(extent) - 1 - axis_at))
    return loudness


def gaussian(key, shape, spread, bound, cuts=(), kind=jnp.bfloat16):
    gain = level_of(key, shape, cuts, -0.22, 0.18) if cuts else 1.0
    array = jax.random.normal(key, shape, jnp.float32) * spread * gain
    return jnp.minimum(jnp.maximum(array, -bound), bound).astype(kind)


def setup_inputs(seed: int = 0) -> dict:
    streams_of = jax.random.split(jax.random.key(seed), 10)
    return {
        "image": gaussian(streams_of[0], (CAMS, C, H, W), 1.0, 6.0, ((0, 32), (2, 4))),
        "conv_first": gaussian(streams_of[1], (C, 9 * C), (9 * C) ** -0.5, 0.5),
        "conv_second": gaussian(streams_of[2], (C, 9 * C), (9 * C) ** -0.5, 0.5),
        "conv_uv": gaussian(streams_of[3], (C, 9 * C), (9 * C) ** -0.5, 0.5),
        "send_block": plant(jax.random.randint(streams_of[4], (CAMS, STRIPS, CAMS * STRIPS, CAP), 0, NB), jax.random.fold_in(streams_of[4], 1), 0, NB - 1).astype(jnp.int32),
        "send_shift": plant(jax.random.randint(streams_of[5], (CAMS, STRIPS, CAMS * STRIPS, CAP), 0, TL), jax.random.fold_in(streams_of[5], 1), 0, TL - 1).astype(jnp.int32),
        "send_weight": plant(jax.random.randint(streams_of[6], (CAMS, STRIPS, CAMS * STRIPS, CAP), 1, 65), jax.random.fold_in(streams_of[6], 1), 1, 64).astype(jnp.int32),
        "send_count": draw_send_count(jax.random.fold_in(streams_of[9], 71), 0),
        "recv_tile": plant(jax.random.randint(streams_of[8], (STRIPS, CAMS, CAMS * STRIPS, CAP), 0, AR_DEV), jax.random.fold_in(streams_of[8], 1), 0, AR_DEV - 1).astype(jnp.int32),
    }


def conv_layer(field, weight):
    channels = field.shape[0]
    height = field.shape[1]
    width = field.shape[2]
    padded = jnp.pad(field.astype(jnp.float32), ((0, 0), (1, 1), (1, 1)))
    kernel_all = weight.astype(jnp.float32)
    total = jnp.zeros((weight.shape[0], height, width), jnp.float32)
    for row_step in range(3):
        for col_step in range(3):
            offset = (row_step * 3 + col_step) * channels
            kernel = kernel_all[:, offset:offset + channels]
            window = padded[:, row_step:row_step + height, col_step:col_step + width]
            total = total + jnp.einsum("oi,ihw->ohw", kernel, window, precision=lax.Precision.HIGHEST)
    return total


def reference(image, conv_first, conv_second, conv_uv, send_block, send_shift, send_weight, send_count, recv_tile):
    def camera(pixels):
        hidden = jax.nn.silu(conv_layer(pixels, conv_first)).astype(jnp.bfloat16)
        return conv_layer(hidden, conv_second).astype(jnp.bfloat16)

    features = lax.map(camera, image)
    sources = CAMS * STRIPS
    per_row = W // TL
    blocks = features.reshape(CAMS, C, STRIPS, H_DEV, per_row, TL).transpose(0, 2, 3, 4, 1, 5).reshape(sources, NB, C, TL)
    flat_block = send_block.reshape(sources, sources, CAP)
    flat_shift = send_shift.reshape(sources, sources, CAP)
    flat_weight = send_weight.reshape(sources, sources, CAP)
    flat_count = send_count.reshape(sources, sources)
    flat_tile = recv_tile.transpose(1, 0, 2, 3).reshape(sources, sources, CAP)
    source_ids = jnp.arange(sources).astype(jnp.int32)
    slot_ids = jnp.arange(CAP).astype(jnp.int32)
    texel_ids = jnp.arange(TL).astype(jnp.int32)

    def owner(region):
        chosen = flat_block[:, region]
        shifts = flat_shift[:, region]
        counts = flat_count[:, region]
        values = blocks[source_ids[:, None], chosen]
        where_from = (texel_ids[None, None, :] - shifts[:, :, None]) % TL
        where_from = jnp.broadcast_to(where_from[:, :, None, :], values.shape).astype(jnp.int32)
        shifted = jnp.take_along_axis(values, where_from, axis=3)
        scales = jnp.where(slot_ids[None, :] < counts[:, None], flat_weight[:, region].astype(jnp.float32) / 16.0, jnp.float32(0.0))
        payload = (shifted.astype(jnp.float32) * scales[:, :, None, None]).astype(jnp.bfloat16)
        scale_wire = scales.astype(jnp.bfloat16)
        tiles = flat_tile[region].reshape(sources * CAP).astype(jnp.int32)
        total = jax.ops.segment_sum(payload.reshape(sources * CAP, C * TL).astype(jnp.float32), tiles, num_segments=AR_DEV)
        weight_sum = jax.ops.segment_sum(scale_wire.reshape(sources * CAP).astype(jnp.float32), tiles, num_segments=AR_DEV)
        joined = (total / jnp.maximum(weight_sum, jnp.float32(1.0))[:, None]).astype(jnp.bfloat16)
        return joined.reshape(AR_DEV, C, TL)

    regions = lax.map(owner, jnp.arange(sources).astype(jnp.int32))
    atlas = regions.reshape(CAMS, STRIPS, AR_DEV, C, TL).transpose(3, 1, 2, 0, 4).reshape(C, AR, AC)
    blended = atlas.astype(jnp.float32) + conv_layer(atlas, conv_uv)
    return blended.astype(jnp.bfloat16)
```

```python
import functools

import jax
import jax.numpy as jnp
from jax import lax
from jax.experimental import pallas as pl
from jax.experimental.pallas import tpu as pltpu
from jax.sharding import PartitionSpec as P

C = 16
W = 2048
TL = 128
CAP = 16
AR_DEV = 1024
PEERS = 128
ROWS = 32
F32 = jnp.float32
BF16 = jnp.bfloat16
MESH = pl.DeviceIdType.MESH
NT = (((1,), (1,)), ((), ()))


def iota(shape, dim):
    return lax.broadcasted_iota(jnp.int32, shape, dim)


def dot(a, b):
    return jnp.dot(a, b, preferred_element_type=F32)


def band(weight, m, k, out_of_m, in_of_k):
    pick = jnp.where(out_of_m(iota((m, C), 0))[0] == iota((m, C), 1), 1.0, 0.0).astype(BF16)
    rows = dot(pick, weight).astype(BF16)
    step = in_of_k(iota((m, k), 1))[1] - out_of_m(iota((m, k), 0))[1] + 1
    channel = in_of_k(iota((9 * C, k), 1))[0]
    source = iota((9 * C, k), 0)
    taps = []
    for b in range(3):
        total = jnp.zeros((m, k), F32)
        for a in range(3):
            spread = jnp.where(source == (3 * a + b) * C + channel, 1.0, 0.0).astype(BF16)
            total = total + jnp.where(step == a, dot(rows, spread), 0.0)
        taps.append(total.astype(BF16))
    return taps


def row_major(first):
    return lambda i: (i % C, i // C + first)


def channel_major(first):
    return lambda i: (i // 16, i % 16 + first)


def shift_add(left, mid, right):
    n = mid.shape[1]
    lane = iota(mid.shape, 1)
    a = jnp.where(lane == 0, 0.0, pltpu.roll(left, 1, 1))
    b = jnp.where(lane == n - 1, 0.0, pltpu.roll(right, n - 1, 1))
    return mid + a + b


def join_kernel(
    image, w1, w2, code, scale_rows, tiles,
    joined, above, below, side_cols, corners,
    band1, band1h, band2, part_a, part_b, part_g, hidden, feats,
    edge_out, edge_in, turned, outbox, inbox, scale_in, onehot, total, wsum, pick_cols, cols, side_in, col_in, row_in,
    edge_send, edge_recv, send_sem, recv_sem, ssend_sem, srecv_sem, hsend, hrecv,
):
    cam = lax.axis_index("cam")
    row = lax.axis_index("row")
    cams = lax.axis_size("cam")
    strips = lax.axis_size("row")
    me = cam * strips + row

    barrier = pltpu.get_barrier_semaphore()

    def greet(i, carry):
        p = lax.rem(me + i, PEERS)
        pl.semaphore_signal(barrier, inc=1, device_id=(p // strips, p % strips), device_id_type=MESH)
        return carry

    lax.fori_loop(1, PEERS, greet, 0)

    def edges(n, carry):
        at = pl.ds(pl.multiple_of(n * 256, 256), 256)
        for half in range(2):
            field = image[:, half * 16 : half * 16 + 16, at].reshape(256, 256)
            first = 14 if half == 1 else 0
            m, k = iota((32, 256), 0), iota((32, 256), 1)
            pick = jnp.where(k == (m % C) * 16 + first + m // C, 1.0, 0.0).astype(BF16)
            edge_out[half, :, at] = dot(pick, field).astype(BF16)
        return carry

    lax.fori_loop(0, W // 256, edges, 0)
    up = (cam, lax.rem(row + strips - 1, strips))
    down = (cam, lax.rem(row + 1, strips))
    pl.semaphore_wait(barrier, PEERS - 1)
    edge_copies = [
        pltpu.make_async_remote_copy(
            src_ref=edge_out.at[half], dst_ref=edge_in.at[half], send_sem=edge_send.at[half], recv_sem=edge_recv.at[half],
            device_id=where, device_id_type=MESH,
        )
        for half, where in ((0, up), (1, down))
    ]
    for copy in edge_copies:
        copy.start()

    for b, taps in enumerate(band(w1[...], 288, 256, row_major(-1), channel_major(0))):
        band1[b] = taps
    for b, taps in enumerate(band(w1[...], 32, 32, row_major(-1), row_major(-2))):
        band1h[0, b] = taps
    for b, taps in enumerate(band(w1[...], 32, 32, row_major(31), row_major(32))):
        band1h[1, b] = taps
    for b, taps in enumerate(band(w2[...], 224, 256, row_major(0), row_major(-1))):
        band2[b] = taps

    def first_main(n, carry):
        at = pl.ds(pl.multiple_of(n * 256, 256), 256)
        for half, part in ((0, part_a), (1, part_b)):
            field = image[:, half * 16 : half * 16 + 16, at].reshape(256, 256)
            for b in range(3):
                part[b, :, at] = dot(band1[b], field)
        return carry

    lax.fori_loop(0, W // 256, first_main, 0)

    def silu(v):
        return v / (1.0 + jnp.exp(-v))

    def hide(at, sources):
        taps = []
        for b in range(3):
            value = None
            for part, first in sources:
                term = part[b, pl.ds(first, 16), :]
                value = term if value is None else value + term
            taps.append(value)
        return silu(shift_add(*taps))

    def put(at, value):
        hidden[pl.ds(at, 16), :] = value.astype(BF16)

    def body_a(i, carry):
        at = pl.multiple_of(i * 16, 16)
        put(at, hide(i, [(part_a, at)]))
        return carry

    def body_b(i, carry):
        at = pl.multiple_of(i * 16, 16)
        put(at, hide(i, [(part_b, pl.multiple_of(at - 256, 16))]))
        return carry

    lax.fori_loop(2, 16, body_a, 0)
    for i in (16, 17):
        put(i * 16, hide(i, [(part_a, i * 16), (part_b, i * 16 - 256)]))
    lax.fori_loop(18, 32, body_b, 0)

    for copy in edge_copies:
        copy.wait()
    has_above = (row > 0).astype(F32)
    has_below = (row < strips - 1).astype(F32)
    above_bf = has_above.astype(BF16)
    below_bf = has_below.astype(BF16)

    def first_edge(n, carry):
        at = pl.ds(pl.multiple_of(n * 256, 256), 256)
        top = edge_in[1, :, at] * above_bf
        bottom = edge_in[0, :, at] * below_bf
        for b in range(3):
            part_g[b, 0:32, at] = dot(band1h[0, b], top)
            part_g[b, 32:64, at] = dot(band1h[1, b], bottom)
        return carry

    lax.fori_loop(0, W // 256, first_edge, 0)
    put(0, hide(0, [(part_a, 0), (part_g, 0)]) * has_above)
    put(16, hide(1, [(part_a, 16), (part_g, 16)]))
    put(512, hide(32, [(part_b, 256), (part_g, 32)]))
    put(528, hide(33, [(part_b, 272), (part_g, 48)]) * has_below)

    def second(n, carry):
        at = pl.ds(pl.multiple_of(n * 256, 256), 256)
        for b in range(3):
            part_a[b, 0:224, at] = dot(band2[b], hidden[0:256, at])
            part_b[b, 0:224, at] = dot(band2[b], hidden[224:480, at])
            part_g[b, :, at] = dot(band2[b, 0:64, 0:96], hidden[448:544, at])
        return carry

    lax.fori_loop(0, W // 256, second, 0)

    def feature_row(part, first):
        def body(i, carry):
            at = pl.ds(pl.multiple_of(i * 16, 16), 16)
            value = shift_add(part[0, at, :], part[1, at, :], part[2, at, :]).astype(BF16).astype(F32)
            for t in range(W // TL):
                feats[(first + i) * (W // TL) + t] = value[:, t * TL : (t + 1) * TL]
            return carry

        return body

    lax.fori_loop(0, 14, feature_row(part_a, 0), 0)
    lax.fori_loop(0, 14, feature_row(part_b, 14), 0)
    lax.fori_loop(0, 4, feature_row(part_g, 28), 0)

    zc = lax.rem(me, 8)
    unit = me // 8
    uy, ux = unit // 4, unit % 4

    def peer_of(step):
        d = lax.rem((step // 8) * 5, 16)
        k = step % 8
        u = lax.rem(uy + d // 4, 4) * 4 + lax.rem(ux + d % 4, 4)
        return u * 8 + lax.rem(zc // 4 + k // 4, 2) * 4 + lax.rem(zc % 4 + k % 4, 4)

    def make(p, slot, put_tile):
        for e in range(CAP):
            word = code[p * CAP + e]
            block = word & 511
            shift = (word >> 9) & 127
            scale = (word >> 16).astype(F32) * 0.0625
            turned[slot, e * C : (e + 1) * C, :] = pltpu.roll(feats[block], shift, 1) * scale
        for q in range(C):
            put_tile(q, turned[slot, pl.ds(q, CAP, stride=C), :].astype(BF16))

    def put_own(q, value):
        inbox[me, q] = value

    make(me, 0, put_own)
    scale_in[me] = scale_rows[me]

    def block_copy(p):
        return pltpu.make_async_remote_copy(
            src_ref=outbox.at[p], dst_ref=inbox.at[me], send_sem=send_sem, recv_sem=recv_sem.at[unit],
            device_id=(p // strips, p % strips), device_id_type=MESH,
        )

    def scale_copy(p):
        return pltpu.make_async_remote_copy(
            src_ref=scale_rows.at[p], dst_ref=scale_in.at[me], send_sem=ssend_sem, recv_sem=srecv_sem,
            device_id=(p // strips, p % strips), device_id_type=MESH,
        )

    def send_step(step, carry):
        p = peer_of(step)

        def put_tile(q, value):
            outbox[p, q] = value

        make(p, lax.rem(step, 2), put_tile)
        scale_copy(p).start()
        block_copy(p).start()
        return carry

    lax.fori_loop(1, PEERS, send_step, 0)

    def pick_body(q, carry):
        j, lane = iota((TL, 256), 0), iota((TL, 256), 1)
        hit = ((j == 0) & (lane == q)) | ((j == TL - 1) & (lane == q + TL))
        pick_cols[pl.ds(pl.multiple_of(q * TL, TL), TL), :] = jnp.where(hit, 1.0, 0.0).astype(BF16)
        return carry

    lax.fori_loop(0, C, pick_body, 0)

    def clear(i, carry):
        total[pl.ds(pl.multiple_of(i * 1024, 1024), 1024), :] = jnp.zeros((1024, TL), F32)
        return carry

    lax.fori_loop(0, C, clear, 0)
    wsum[...] = jnp.zeros_like(wsum)

    pltpu.make_async_remote_copy(
        src_ref=scale_rows.at[pl.ds(0, PEERS - 1)], dst_ref=scale_in.at[pl.ds(0, PEERS - 1)], send_sem=ssend_sem,
        recv_sem=srecv_sem, device_id=up, device_id_type=MESH,
    ).wait()

    def wait_unit(u, count):
        pltpu.make_async_remote_copy(
            src_ref=outbox.at[pl.ds(0, count)], dst_ref=inbox.at[pl.ds(0, count)], send_sem=send_sem,
            recv_sem=recv_sem.at[u], device_id=up, device_id_type=MESH,
        ).wait_recv()

    def source_unit(i):
        d = lax.rem(i * 5, 16)
        return lax.rem(uy + 4 - d // 4, 4) * 4 + lax.rem(ux + 4 - d % 4, 4)

    def add_pair(i):
        u, v = source_unit(2 * i), source_unit(2 * i + 1)
        ids = jnp.concatenate([tiles[pl.ds(u, 1), :], tiles[pl.ds(v, 1), :]], axis=1)
        weights = jnp.concatenate(
            [jnp.sum(scale_in[pl.ds(u * 8, 8)], axis=0), jnp.sum(scale_in[pl.ds(v * 8, 8)], axis=0)], axis=1
        )
        weights = jnp.broadcast_to(weights, (TL, 256)).astype(BF16)

        def mark(m, carry):
            at = pl.ds(pl.multiple_of(m * 256, 256), 256)
            hot = jnp.where(iota((256, 256), 0) + m * 256 == ids, 1.0, 0.0).astype(BF16)
            onehot[at, :] = hot
            wsum[at, :] += lax.dot_general(hot, weights, NT, preferred_element_type=F32)
            return carry

        lax.fori_loop(0, 4, mark, 0)

        def channels(t, carry):
            cols = []
            for q in (2 * t, 2 * t + 1):
                cols.append(
                    jnp.concatenate(
                        [inbox[pl.ds(u * 8, 8), q].reshape(TL, TL), inbox[pl.ds(v * 8, 8), q].reshape(TL, TL)], axis=0
                    )
                )
            block = jnp.concatenate(cols, axis=1)
            for m in range(4):
                got = dot(onehot[m * 256 : (m + 1) * 256, :], block)
                for h in range(2):
                    at = pl.ds(pl.multiple_of((2 * t + h) * AR_DEV + m * 256, 256), 256)
                    total[at, :] += got[:, h * TL : (h + 1) * TL]
            return carry

        lax.fori_loop(0, C // 2, channels, 0)

    wait_unit(source_unit(0), 7)
    wait_unit(source_unit(1), 8)
    add_pair(0)

    def receive(i, carry):
        wait_unit(source_unit(2 * i), 8)
        wait_unit(source_unit(2 * i + 1), 8)
        add_pair(i)
        return carry

    lax.fori_loop(1, 8, receive, 0)

    wsum[...] = 1.0 / jnp.maximum(wsum[...], 1.0)

    def ends(g, carry):
        for last in range(2):
            r = g * 16 + 15 * last
            value = (total[pl.ds(r, C, stride=AR_DEV), :] * wsum[pl.ds(r, 1), :]).astype(BF16)
            if last:
                above[g + 1] = value
            else:
                below[g] = value
        return carry

    lax.fori_loop(0, 64, ends, 0)

    def normal(rb, carry):
        at = pl.ds(pl.multiple_of(rb * TL, TL), TL)
        inverse = wsum[at, :]
        parts = []
        for q in range(C):
            value = (total[pl.ds(pl.multiple_of(q * AR_DEV + rb * TL, TL), TL), :] * inverse).astype(BF16)
            joined[q, at, :] = value
            parts.append(value)
        picked = dot(jnp.concatenate(parts, axis=1), pick_cols[...])
        left = pltpu.roll(picked[:, :TL], rb * C, 1)
        right = pltpu.roll(picked[:, TL:], rb * C, 1)
        return carry[0] + left, carry[1] + right

    zero = jnp.zeros((TL, TL), F32)
    left, right = lax.fori_loop(0, AR_DEV // TL, normal, (zero, zero))
    cols[0] = left.astype(BF16)
    cols[1] = right.astype(BF16)

    west, east = lax.rem(cam + cams - 1, cams), lax.rem(cam + 1, cams)
    north, south = lax.rem(row + strips - 1, strips), lax.rem(row + 1, strips)
    plan = [
        (cols.at[1], side_in.at[0], (east, row)),
        (cols.at[0], side_in.at[1], (west, row)),
        (above.at[64], row_in.at[0], (cam, south)),
        (below.at[0], row_in.at[1], (cam, north)),
        (cols.at[1, pl.ds(112, 16)], col_in.at[0], (east, south)),
        (cols.at[1, pl.ds(0, 16)], col_in.at[1], (east, north)),
        (cols.at[0, pl.ds(112, 16)], col_in.at[2], (west, south)),
        (cols.at[0, pl.ds(0, 16)], col_in.at[3], (west, north)),
    ]
    copies = [
        pltpu.make_async_remote_copy(
            src_ref=src, dst_ref=dst, send_sem=hsend.at[i], recv_sem=hrecv.at[i], device_id=where, device_id_type=MESH
        )
        for i, (src, dst, where) in enumerate(plan)
    ]
    for copy in copies:
        copy.start()
    pltpu.make_async_remote_copy(
        src_ref=outbox.at[pl.ds(0, PEERS - 1)], dst_ref=inbox.at[pl.ds(0, PEERS - 1)], send_sem=send_sem,
        recv_sem=recv_sem.at[0], device_id=up, device_id_type=MESH,
    ).wait_send()
    for copy in copies:
        copy.wait()
    has_west = (cam > 0).astype(F32)
    has_east = (cam < cams - 1).astype(F32)
    side_cols[0] = side_in[0] * has_west.astype(BF16)
    side_cols[1] = side_in[1] * has_east.astype(BF16)
    above[0] = row_in[0] * above_bf
    below[64] = row_in[1] * below_bf
    for i, factor in enumerate(
        (has_west * has_above, has_west * has_below, has_east * has_above, has_east * has_below)
    ):
        corners[i] = col_in[i] * factor.astype(BF16)


def uv_kernel(weight, joined, above, below, side_cols, corners, texture, bands, delta):
    rb = pl.program_id(0)

    @pl.when(rb == 0)
    def _():
        def out_of(i):
            return i // 16, i % 16

        def in_of(i):
            late = i - 256
            return (
                jnp.where(i < 256, i // 16, late % C),
                jnp.where(i < 256, i % 16, jnp.where(late < C, -1, 16)),
            )

        for b, taps in enumerate(band(weight[...], 256, 288, out_of, in_of)):
            bands[b * 256 : (b + 1) * 256, :] = taps

        lane = iota((TL, TL), 1)
        sub = iota((TL, TL), 0)
        pick = jnp.where(iota((TL, C), 0) % C == iota((TL, C), 1), 1.0, 0.0).astype(BF16)
        rows = dot(pick, weight[...]).astype(BF16)
        for side in range(2):
            own = side_cols[side].astype(F32)
            top = corners[2 * side].astype(F32)[15:16, :]
            bottom = corners[2 * side + 1].astype(F32)[0:1, :]
            before = jnp.where(lane[0:1] >= TL - C, top, own[TL - 1 : TL, :])
            before = pltpu.roll(jnp.broadcast_to(before, (TL, TL)), C, 1)
            after = jnp.where(lane[0:1] < C, bottom, own[0:1, :])
            after = pltpu.roll(jnp.broadcast_to(after, (TL, TL)), TL - C, 1)
            shifted = (
                jnp.where(sub == 0, before, pltpu.roll(own, 1, 0)),
                own,
                jnp.where(sub == TL - 1, after, pltpu.roll(own, TL - 1, 0)),
            )
            result = jnp.zeros((TL, TL), F32)
            for a in range(3):
                source = iota((9 * C, TL), 0)
                spread = jnp.where(source == (3 * a + 2 * side) * C + iota((9 * C, TL), 1) % C, 1.0, 0.0).astype(BF16)
                matrix = jnp.where(sub // C == lane // C, dot(rows, spread), 0.0).astype(BF16)
                result = result + lax.dot_general(shifted[a].astype(BF16), matrix, NT, preferred_element_type=F32)
            delta[side] = result

    turn = lax.rem(TL - rb * C, TL)
    left = pltpu.roll(delta[0], turn, 1)
    right = pltpu.roll(delta[1], turn, 1)
    lane = iota((16, TL), 1)
    for pair in range(4):
        fields = []
        for h in range(2):
            g = pair * 2 + h
            at = rb * 8 + g
            fields.append(
                jnp.concatenate(
                    [joined[:, g * 16 : (g + 1) * 16, :].reshape(256, TL), above[at], below[at + 1]], axis=0
                )
            )
        taps = dot(bands[...], jnp.concatenate(fields, axis=1))
        for h in range(2):
            g = pair * 2 + h
            cut = slice(h * TL, (h + 1) * TL)
            a = pltpu.roll(taps[0:256, cut], 1, 1)
            m = taps[256:512, cut]
            b = pltpu.roll(taps[512:768, cut], TL - 1, 1)
            for o in range(C):
                rows = slice(o * 16, (o + 1) * 16)
                here = slice(g * 16, (g + 1) * 16)
                low = jnp.where(lane == 0, left[here, o : o + 1], a[rows])
                high = jnp.where(lane == TL - 1, right[here, o : o + 1], b[rows])
                value = joined[o, here, :].astype(F32) + m[rows] + low + high
                texture[o, here, :] = value.astype(BF16)


def local(image, conv_first, conv_second, conv_uv, send_block, send_shift, send_weight, send_count, recv_tile):
    me = lax.axis_index("cam") * lax.axis_size("row") + lax.axis_index("row")
    block = send_block.reshape(PEERS, CAP)
    shift = send_shift.reshape(PEERS, CAP)
    valid = lax.broadcasted_iota(jnp.int32, (PEERS, CAP), 1) < send_count.reshape(PEERS, 1)
    weight = jnp.where(valid, send_weight.reshape(PEERS, CAP), 0)
    code = (block + shift * 512 + weight * 65536).reshape(PEERS * CAP)
    scale = weight.astype(F32) * 0.0625
    lane = lax.broadcasted_iota(jnp.int32, (PEERS, TL), 1)
    scale_rows = jnp.where(lane // CAP == me % 8, jnp.tile(scale, (1, 8)), 0.0).reshape(PEERS, 1, TL)
    tiles = recv_tile.reshape(16, TL)

    vmem = pl.BlockSpec(memory_space=pltpu.VMEM)
    smem = pl.BlockSpec(memory_space=pltpu.SMEM)
    dma = pltpu.SemaphoreType.DMA
    joined, above, below, side_cols, corners = pl.pallas_call(
        join_kernel,
        out_shape=[
            jax.ShapeDtypeStruct((C, AR_DEV, TL), BF16),
            jax.ShapeDtypeStruct((65, C, TL), BF16),
            jax.ShapeDtypeStruct((65, C, TL), BF16),
            jax.ShapeDtypeStruct((2, TL, TL), BF16),
            jax.ShapeDtypeStruct((4, 16, TL), BF16),
        ],
        in_specs=[vmem, vmem, vmem, smem, vmem, vmem],
        out_specs=[vmem] * 5,
        scratch_shapes=[
            pltpu.VMEM((3, 288, 256), BF16),
            pltpu.VMEM((2, 3, 32, 32), BF16),
            pltpu.VMEM((3, 224, 256), BF16),
            pltpu.VMEM((3, 288, W), F32),
            pltpu.VMEM((3, 288, W), F32),
            pltpu.VMEM((3, 64, W), F32),
            pltpu.VMEM((544, W), BF16),
            pltpu.VMEM((512, C, TL), F32),
            pltpu.VMEM((2, 32, W), BF16),
            pltpu.VMEM((2, 32, W), BF16),
            pltpu.VMEM((2, CAP * C, TL), F32),
            pltpu.VMEM((PEERS, C, CAP, TL), BF16),
            pltpu.VMEM((PEERS, C, CAP, TL), BF16),
            pltpu.VMEM((PEERS, 1, TL), F32),
            pltpu.VMEM((AR_DEV, 256), BF16),
            pltpu.VMEM((C * AR_DEV, TL), F32),
            pltpu.VMEM((AR_DEV, TL), F32),
            pltpu.VMEM((C * TL, 256), BF16),
            pltpu.VMEM((2, TL, TL), BF16),
            pltpu.VMEM((2, TL, TL), BF16),
            pltpu.VMEM((4, 16, TL), BF16),
            pltpu.VMEM((2, C, TL), BF16),
            dma((2,)), dma((2,)), dma, dma((16,)), dma, dma, dma((8,)), dma((8,)),
        ],
        compiler_params=pltpu.CompilerParams(
            collective_id=0, has_side_effects=True, vmem_limit_bytes=62 * 1024 * 1024
        ),
        cost_estimate=pl.CostEstimate(flops=2 * 10**10, bytes_accessed=3 * 10**7, transcendentals=10**6),
    )(image.reshape(C, ROWS, W), conv_first, conv_second, code, scale_rows, tiles)

    full = lambda shape: pl.BlockSpec(shape, lambda i: (0,) * len(shape))
    return pl.pallas_call(
        uv_kernel,
        out_shape=jax.ShapeDtypeStruct((C, AR_DEV, TL), BF16),
        grid=(AR_DEV // TL,),
        in_specs=[
            full((C, 9 * C)),
            pl.BlockSpec((C, TL, TL), lambda i: (0, i, 0)),
            full((65, C, TL)),
            full((65, C, TL)),
            full((2, TL, TL)),
            full((4, 16, TL)),
        ],
        out_specs=pl.BlockSpec((C, TL, TL), lambda i: (0, i, 0)),
        scratch_shapes=[pltpu.VMEM((768, 288), BF16), pltpu.VMEM((2, TL, TL), F32)],
        compiler_params=pltpu.CompilerParams(vmem_limit_bytes=32 * 1024 * 1024),
        cost_estimate=pl.CostEstimate(flops=10**10, bytes_accessed=10**7, transcendentals=0),
    )(conv_uv, joined, above, below, side_cols, corners)


def solution(mesh):
    return jax.shard_map(
        local,
        mesh=mesh,
        in_specs=(
            P("cam", None, "row", None),
            P(),
            P(),
            P(),
            P("cam", "row", None, None),
            P("cam", "row", None, None),
            P("cam", "row", None, None),
            P("cam", "row", None),
            P("row", "cam", None, None),
        ),
        out_specs=P(None, "row", "cam"),
        check_vma=False,
    )
```

```python
import functools

import jax
import jax.numpy as jnp
from jax import lax
from jax.experimental import pallas as pl
from jax.experimental.pallas import tpu as pltpu
from jax.sharding import PartitionSpec as P

C = 16
W = 2048
TL = 128
CAP = 16
AR_DEV = 1024
PEERS = 128
GROUP = 16
ROWS = 32
F32 = jnp.float32
BF16 = jnp.bfloat16
MESH = pl.DeviceIdType.MESH
NT = (((1,), (1,)), ((), ()))


def iota(shape, dim):
    return lax.broadcasted_iota(jnp.int32, shape, dim)


def dot(a, b):
    return jnp.dot(a, b, preferred_element_type=F32)


def band(weight, m, k, out_of_m, in_of_k):
    pick = jnp.where(out_of_m(iota((m, C), 0))[0] == iota((m, C), 1), 1.0, 0.0).astype(BF16)
    rows = dot(pick, weight).astype(BF16)
    step = in_of_k(iota((m, k), 1))[1] - out_of_m(iota((m, k), 0))[1] + 1
    channel = in_of_k(iota((9 * C, k), 1))[0]
    source = iota((9 * C, k), 0)
    taps = []
    for b in range(3):
        total = jnp.zeros((m, k), F32)
        for a in range(3):
            spread = jnp.where(source == (3 * a + b) * C + channel, 1.0, 0.0).astype(BF16)
            total = total + jnp.where(step == a, dot(rows, spread), 0.0)
        taps.append(total.astype(BF16))
    return taps


def row_major(first):
    return lambda i: (i % C, i // C + first)


def channel_major(first):
    return lambda i: (i // 16, i % 16 + first)


def shift_add(left, mid, right):
    n = mid.shape[1]
    lane = iota(mid.shape, 1)
    a = jnp.where(lane == 0, 0.0, pltpu.roll(left, 1, 1))
    b = jnp.where(lane == n - 1, 0.0, pltpu.roll(right, n - 1, 1))
    return mid + a + b


def join_kernel(
    image, w1, w2, code, scale_rows, tiles,
    joined, above, below, side_cols, corners,
    band1, band1h, band2, part_a, part_b, part_g, hidden, feats,
    edge_out, edge_in, turned, outbox, inbox, scale_in, onehot, total, wsum, pick_cols, cols, side_in, col_in, row_in,
    edge_send, edge_recv, send_sem, recv_sem, ssend_sem, srecv_sem, hsend, hrecv,
):
    cam = lax.axis_index("cam")
    row = lax.axis_index("row")
    cams = lax.axis_size("cam")
    strips = lax.axis_size("row")
    me = cam * strips + row

    barrier = pltpu.get_barrier_semaphore()

    def greet(i, carry):
        p = lax.rem(me + i, PEERS)
        pl.semaphore_signal(barrier, inc=1, device_id=(p // strips, p % strips), device_id_type=MESH)
        return carry

    lax.fori_loop(1, PEERS, greet, 0)

    def edges(n, carry):
        at = pl.ds(pl.multiple_of(n * 256, 256), 256)
        for half in range(2):
            field = image[:, half * 16 : half * 16 + 16, at].reshape(256, 256)
            first = 14 if half == 1 else 0
            m, k = iota((32, 256), 0), iota((32, 256), 1)
            pick = jnp.where(k == (m % C) * 16 + first + m // C, 1.0, 0.0).astype(BF16)
            edge_out[half, :, at] = dot(pick, field).astype(BF16)
        return carry

    lax.fori_loop(0, W // 256, edges, 0)
    up = (cam, lax.rem(row + strips - 1, strips))
    down = (cam, lax.rem(row + 1, strips))
    for b, taps in enumerate(band(w1[...], 288, 256, row_major(-1), channel_major(0))):
        band1[b] = taps
    for b, taps in enumerate(band(w1[...], 32, 32, row_major(-1), row_major(-2))):
        band1h[0, b] = taps
    for b, taps in enumerate(band(w1[...], 32, 32, row_major(31), row_major(32))):
        band1h[1, b] = taps
    for b, taps in enumerate(band(w2[...], 224, 256, row_major(0), row_major(-1))):
        band2[b] = taps

    def first_main(n, carry):
        at = pl.ds(pl.multiple_of(n * 256, 256), 256)
        for half, part in ((0, part_a), (1, part_b)):
            field = image[:, half * 16 : half * 16 + 16, at].reshape(256, 256)
            for b in range(3):
                part[b, :, at] = dot(band1[b], field)
        return carry

    lax.fori_loop(0, W // 256, first_main, 0)
    pl.semaphore_wait(barrier, PEERS - 1)
    edge_copies = [
        pltpu.make_async_remote_copy(
            src_ref=edge_out.at[half], dst_ref=edge_in.at[half], send_sem=edge_send.at[half], recv_sem=edge_recv.at[half],
            device_id=where, device_id_type=MESH,
        )
        for half, where in ((0, up), (1, down))
    ]
    for copy in edge_copies:
        copy.start()


    def silu(v):
        return v / (1.0 + jnp.exp(-v))

    def hide(at, sources):
        taps = []
        for b in range(3):
            value = None
            for part, first in sources:
                term = part[b, pl.ds(first, 16), :]
                value = term if value is None else value + term
            taps.append(value)
        return silu(shift_add(*taps))

    def put(at, value):
        hidden[pl.ds(at, 16), :] = value.astype(BF16)

    def body_a(i, carry):
        at = pl.multiple_of(i * 16, 16)
        put(at, hide(i, [(part_a, at)]))
        return carry

    def body_b(i, carry):
        at = pl.multiple_of(i * 16, 16)
        put(at, hide(i, [(part_b, pl.multiple_of(at - 256, 16))]))
        return carry

    lax.fori_loop(2, 16, body_a, 0)
    for i in (16, 17):
        put(i * 16, hide(i, [(part_a, i * 16), (part_b, i * 16 - 256)]))
    lax.fori_loop(18, 32, body_b, 0)

    for copy in edge_copies:
        copy.wait()
    has_above = (row > 0).astype(F32)
    has_below = (row < strips - 1).astype(F32)
    above_bf = has_above.astype(BF16)
    below_bf = has_below.astype(BF16)

    def first_edge(n, carry):
        at = pl.ds(pl.multiple_of(n * 256, 256), 256)
        top = edge_in[1, :, at] * above_bf
        bottom = edge_in[0, :, at] * below_bf
        for b in range(3):
            part_g[b, 0:32, at] = dot(band1h[0, b], top)
            part_g[b, 32:64, at] = dot(band1h[1, b], bottom)
        return carry

    lax.fori_loop(0, W // 256, first_edge, 0)
    put(0, hide(0, [(part_a, 0), (part_g, 0)]) * has_above)
    put(16, hide(1, [(part_a, 16), (part_g, 16)]))
    put(512, hide(32, [(part_b, 256), (part_g, 32)]))
    put(528, hide(33, [(part_b, 272), (part_g, 48)]) * has_below)

    def second(n, carry):
        at = pl.ds(pl.multiple_of(n * 256, 256), 256)
        for b in range(3):
            part_a[b, 0:224, at] = dot(band2[b], hidden[0:256, at])
            part_b[b, 0:224, at] = dot(band2[b], hidden[224:480, at])
            part_g[b, :, at] = dot(band2[b, 0:64, 0:96], hidden[448:544, at])
        return carry

    lax.fori_loop(0, W // 256, second, 0)

    def feature_row(part, first):
        def body(i, carry):
            at = pl.ds(pl.multiple_of(i * 16, 16), 16)
            value = shift_add(part[0, at, :], part[1, at, :], part[2, at, :]).astype(BF16).astype(F32)
            for t in range(W // TL):
                feats[(first + i) * (W // TL) + t] = value[:, t * TL : (t + 1) * TL]
            return carry

        return body

    lax.fori_loop(0, 14, feature_row(part_a, 0), 0)
    lax.fori_loop(0, 14, feature_row(part_b, 14), 0)
    lax.fori_loop(0, 4, feature_row(part_g, 28), 0)

    my, mx, mc = cam // 8, lax.rem(cam // 2, 4), lax.rem(cam, 2)

    def offset(t):
        i, c, b = t % 4, (t // 8) % 4, t // 32

        def order(v):
            w = lax.rem(v, 4)
            return lax.rem(2 * w, 3) + 3 * (w // 3)

        return order(i + b), order(i), (t // 4) % 2, order(i + c)

    def moved(core, sign, t):
        dy, dx, _, dz = offset(t)
        place = (lax.rem(my + 4 + sign * dy, 4) * 4 + lax.rem(mx + 4 + sign * dx, 4)) * 2 + core
        return place * 4 + lax.rem(row + 4 + sign * dz, 4)

    def peer_of(t):
        return moved(lax.rem(mc + offset(t)[2], 2), 1 - 2 * mc, t)

    def source_of(t):
        core = lax.rem(mc + offset(t)[2], 2)
        return moved(core, 2 * core - 1, t)

    def make(p, slot, put_tile):
        for e in range(CAP):
            word = code[p * CAP + e]
            block = word & 511
            shift = (word >> 9) & 127
            scale = (word >> 16).astype(F32) * 0.0625
            turned[slot, e * C : (e + 1) * C, :] = pltpu.roll(feats[block], shift, 1) * scale
        for q in range(C):
            put_tile(q, turned[slot, pl.ds(q, CAP, stride=C), :].astype(BF16))

    def put_own(q, value):
        inbox[0, q] = value

    make(me, 0, put_own)
    scale_in[0] = scale_rows[me]

    def block_copy(t, p):
        return pltpu.make_async_remote_copy(
            src_ref=outbox.at[t], dst_ref=inbox.at[t], send_sem=send_sem,
            recv_sem=recv_sem.at[t // GROUP], device_id=(p // strips, p % strips), device_id_type=MESH,
        )

    def scale_copy(t, p):
        return pltpu.make_async_remote_copy(
            src_ref=scale_rows.at[p], dst_ref=scale_in.at[t], send_sem=ssend_sem, recv_sem=srecv_sem,
            device_id=(p // strips, p % strips), device_id_type=MESH,
        )

    def send_step(t, carry):
        p = peer_of(t)

        def put_tile(q, value):
            outbox[t, q] = value

        make(p, lax.rem(t, 2), put_tile)

        scale_copy(t, p).start()
        block_copy(t, p).start()
        return carry

    lax.fori_loop(1, PEERS, send_step, 0)

    def pick_body(q, carry):
        j, lane = iota((TL, 256), 0), iota((TL, 256), 1)
        hit = ((j == 0) & (lane == q)) | ((j == TL - 1) & (lane == q + TL))
        pick_cols[pl.ds(pl.multiple_of(q * TL, TL), TL), :] = jnp.where(hit, 1.0, 0.0).astype(BF16)
        return carry

    lax.fori_loop(0, C, pick_body, 0)

    def clear(i, carry):
        total[pl.ds(pl.multiple_of(i * 1024, 1024), 1024), :] = jnp.zeros((1024, TL), F32)
        return carry

    lax.fori_loop(0, C, clear, 0)
    wsum[...] = jnp.zeros_like(wsum)

    def wait_group(g, count):
        pltpu.make_async_remote_copy(
            src_ref=outbox.at[pl.ds(0, count)], dst_ref=inbox.at[pl.ds(0, count)], send_sem=send_sem,
            recv_sem=recv_sem.at[g], device_id=up, device_id_type=MESH,
        ).wait_recv()

    def lanes_of(ref, g, half):
        first = g * GROUP + half * 8
        lane = iota((1, TL), 1) // CAP
        value = jnp.zeros((1, TL), ref.dtype)
        for i in range(8):
            index = first + i if ref is scale_in else source_of(first + i)
            value = jnp.where(lane == i, ref[index], value)
        return value

    def mark_group(g, carry):
        ids = jnp.concatenate([lanes_of(tiles, g, 0), lanes_of(tiles, g, 1)], axis=1)
        for m in range(4):
            hot = jnp.where(iota((256, 256), 0) + m * 256 == ids, 1.0, 0.0).astype(BF16)
            onehot[g, m * 256 : (m + 1) * 256, :] = hot
        return carry

    def weigh_group(g, carry):
        weights = jnp.concatenate([lanes_of(scale_in, g, 0), lanes_of(scale_in, g, 1)], axis=1)
        weights = jnp.broadcast_to(weights, (TL, 256)).astype(BF16)
        for m in range(4):
            at = slice(m * 256, (m + 1) * 256)
            wsum[at, :] += lax.dot_general(onehot[g, at, :], weights, NT, preferred_element_type=F32)
        return carry

    def group_sum(g, t, m):
        block = jnp.concatenate(
            [inbox[pl.ds(g * GROUP, GROUP), 2 * t + h].reshape(256, TL) for h in range(2)], axis=1
        )
        return dot(onehot[g, m * 256 : (m + 1) * 256, :], block)

    def add_group(g):
        def channels(t, carry):
            for m in range(4):
                got = group_sum(g, t, m)
                for h in range(2):
                    at = pl.ds(pl.multiple_of((2 * t + h) * AR_DEV + m * 256, 256), 256)
                    total[at, :] += got[:, h * TL : (h + 1) * TL]
            return carry

        lax.fori_loop(0, C // 2, channels, 0)

    lax.fori_loop(0, PEERS // GROUP, mark_group, 0)
    wait_group(0, GROUP - 1)
    add_group(0)

    def receive(g, carry):
        wait_group(g, GROUP)
        add_group(g)
        return carry

    last = PEERS // GROUP - 1
    lax.fori_loop(1, last, receive, 0)
    pltpu.make_async_remote_copy(
        src_ref=scale_rows.at[pl.ds(0, PEERS - 1)], dst_ref=scale_in.at[pl.ds(0, PEERS - 1)], send_sem=ssend_sem,
        recv_sem=srecv_sem, device_id=up, device_id_type=MESH,
    ).wait()
    lax.fori_loop(0, PEERS // GROUP, weigh_group, 0)
    wsum[...] = 1.0 / jnp.maximum(wsum[...], 1.0)
    wait_group(last, GROUP)

    def finish(t, carry):
        for m in range(4):
            got = group_sum(last, t, m)
            for h in range(2):
                at = pl.ds(pl.multiple_of((2 * t + h) * AR_DEV + m * 256, 256), 256)
                value = (total[at, :] + got[:, h * TL : (h + 1) * TL]) * wsum[m * 256 : (m + 1) * 256, :]
                total[at, :] = value
                joined[2 * t + h, m * 256 : (m + 1) * 256, :] = value.astype(BF16)
        return carry

    lax.fori_loop(0, C // 2, finish, 0)

    def ends(g, carry):
        for last in range(2):
            r = g * 16 + 15 * last
            value = total[pl.ds(r, C, stride=AR_DEV), :].astype(BF16)
            if last:
                above[g + 1] = value
            else:
                below[g] = value
        return carry

    lax.fori_loop(0, 64, ends, 0)

    def normal(rb, carry):
        at = pl.ds(pl.multiple_of(rb * TL, TL), TL)
        parts = [joined[q, at, :] for q in range(C)]
        picked = dot(jnp.concatenate(parts, axis=1), pick_cols[...])
        left = pltpu.roll(picked[:, :TL], rb * C, 1)
        right = pltpu.roll(picked[:, TL:], rb * C, 1)
        return carry[0] + left, carry[1] + right

    zero = jnp.zeros((TL, TL), F32)
    left, right = lax.fori_loop(0, AR_DEV // TL, normal, (zero, zero))
    cols[0] = left.astype(BF16)
    cols[1] = right.astype(BF16)

    west, east = lax.rem(cam + cams - 1, cams), lax.rem(cam + 1, cams)
    north, south = lax.rem(row + strips - 1, strips), lax.rem(row + 1, strips)
    plan = [
        (cols.at[1], side_in.at[0], (east, row)),
        (cols.at[0], side_in.at[1], (west, row)),
        (above.at[64], row_in.at[0], (cam, south)),
        (below.at[0], row_in.at[1], (cam, north)),
        (cols.at[1, pl.ds(112, 16)], col_in.at[0], (east, south)),
        (cols.at[1, pl.ds(0, 16)], col_in.at[1], (east, north)),
        (cols.at[0, pl.ds(112, 16)], col_in.at[2], (west, south)),
        (cols.at[0, pl.ds(0, 16)], col_in.at[3], (west, north)),
    ]
    copies = [
        pltpu.make_async_remote_copy(
            src_ref=src, dst_ref=dst, send_sem=hsend.at[i], recv_sem=hrecv.at[i], device_id=where, device_id_type=MESH
        )
        for i, (src, dst, where) in enumerate(plan)
    ]
    for copy in copies:
        copy.start()
    pltpu.make_async_remote_copy(
        src_ref=outbox.at[pl.ds(0, PEERS - 1)], dst_ref=inbox.at[pl.ds(0, PEERS - 1)], send_sem=send_sem,
        recv_sem=recv_sem.at[0], device_id=up, device_id_type=MESH,
    ).wait_send()
    for copy in copies:
        copy.wait()
    has_west = (cam > 0).astype(F32)
    has_east = (cam < cams - 1).astype(F32)
    side_cols[0] = side_in[0] * has_west.astype(BF16)
    side_cols[1] = side_in[1] * has_east.astype(BF16)
    above[0] = row_in[0] * above_bf
    below[64] = row_in[1] * below_bf
    for i, factor in enumerate(
        (has_west * has_above, has_west * has_below, has_east * has_above, has_east * has_below)
    ):
        corners[i] = col_in[i] * factor.astype(BF16)


def uv_kernel(weight, joined, above, below, side_cols, corners, texture, bands, delta):
    rb = pl.program_id(0)

    @pl.when(rb == 0)
    def _():
        def out_of(i):
            return i // 16, i % 16

        def in_of(i):
            late = i - 256
            return (
                jnp.where(i < 256, i // 16, late % C),
                jnp.where(i < 256, i % 16, jnp.where(late < C, -1, 16)),
            )

        for b, taps in enumerate(band(weight[...], 256, 288, out_of, in_of)):
            bands[b * 256 : (b + 1) * 256, :] = taps

        lane = iota((TL, TL), 1)
        sub = iota((TL, TL), 0)
        pick = jnp.where(iota((TL, C), 0) % C == iota((TL, C), 1), 1.0, 0.0).astype(BF16)
        rows = dot(pick, weight[...]).astype(BF16)
        for side in range(2):
            own = side_cols[side].astype(F32)
            top = corners[2 * side].astype(F32)[15:16, :]
            bottom = corners[2 * side + 1].astype(F32)[0:1, :]
            before = jnp.where(lane[0:1] >= TL - C, top, own[TL - 1 : TL, :])
            before = pltpu.roll(jnp.broadcast_to(before, (TL, TL)), C, 1)
            after = jnp.where(lane[0:1] < C, bottom, own[0:1, :])
            after = pltpu.roll(jnp.broadcast_to(after, (TL, TL)), TL - C, 1)
            shifted = (
                jnp.where(sub == 0, before, pltpu.roll(own, 1, 0)),
                own,
                jnp.where(sub == TL - 1, after, pltpu.roll(own, TL - 1, 0)),
            )
            result = jnp.zeros((TL, TL), F32)
            for a in range(3):
                source = iota((9 * C, TL), 0)
                spread = jnp.where(source == (3 * a + 2 * side) * C + iota((9 * C, TL), 1) % C, 1.0, 0.0).astype(BF16)
                matrix = jnp.where(sub // C == lane // C, dot(rows, spread), 0.0).astype(BF16)
                result = result + lax.dot_general(shifted[a].astype(BF16), matrix, NT, preferred_element_type=F32)
            delta[side] = result

    turn = lax.rem(TL - rb * C, TL)
    left = pltpu.roll(delta[0], turn, 1)
    right = pltpu.roll(delta[1], turn, 1)
    lane = iota((16, TL), 1)
    for pair in range(4):
        fields = []
        for h in range(2):
            g = pair * 2 + h
            at = rb * 8 + g
            fields.append(
                jnp.concatenate(
                    [joined[:, g * 16 : (g + 1) * 16, :].reshape(256, TL), above[at], below[at + 1]], axis=0
                )
            )
        taps = dot(bands[...], jnp.concatenate(fields, axis=1))
        for h in range(2):
            g = pair * 2 + h
            cut = slice(h * TL, (h + 1) * TL)
            a = pltpu.roll(taps[0:256, cut], 1, 1)
            m = taps[256:512, cut]
            b = pltpu.roll(taps[512:768, cut], TL - 1, 1)
            for o in range(C):
                rows = slice(o * 16, (o + 1) * 16)
                here = slice(g * 16, (g + 1) * 16)
                low = jnp.where(lane == 0, left[here, o : o + 1], a[rows])
                high = jnp.where(lane == TL - 1, right[here, o : o + 1], b[rows])
                value = joined[o, here, :].astype(F32) + m[rows] + low + high
                texture[o, here, :] = value.astype(BF16)


def local(image, conv_first, conv_second, conv_uv, send_block, send_shift, send_weight, send_count, recv_tile):
    block = send_block.reshape(PEERS, CAP)
    shift = send_shift.reshape(PEERS, CAP)
    valid = lax.broadcasted_iota(jnp.int32, (PEERS, CAP), 1) < send_count.reshape(PEERS, 1)
    weight = jnp.where(valid, send_weight.reshape(PEERS, CAP), 0)
    code = (block + shift * 512 + weight * 65536).reshape(PEERS * CAP)
    scale = weight.astype(F32) * 0.0625
    scale_rows = jnp.tile(scale, (1, 8)).reshape(PEERS, 1, TL)
    tiles = jnp.tile(recv_tile.reshape(PEERS, CAP), (1, 8)).reshape(PEERS, 1, TL)

    vmem = pl.BlockSpec(memory_space=pltpu.VMEM)
    smem = pl.BlockSpec(memory_space=pltpu.SMEM)
    dma = pltpu.SemaphoreType.DMA
    joined, above, below, side_cols, corners = pl.pallas_call(
        join_kernel,
        out_shape=[
            jax.ShapeDtypeStruct((C, AR_DEV, TL), BF16),
            jax.ShapeDtypeStruct((65, C, TL), BF16),
            jax.ShapeDtypeStruct((65, C, TL), BF16),
            jax.ShapeDtypeStruct((2, TL, TL), BF16),
            jax.ShapeDtypeStruct((4, 16, TL), BF16),
        ],
        in_specs=[vmem, vmem, vmem, smem, vmem, vmem],
        out_specs=[vmem] * 5,
        scratch_shapes=[
            pltpu.VMEM((3, 288, 256), BF16),
            pltpu.VMEM((2, 3, 32, 32), BF16),
            pltpu.VMEM((3, 224, 256), BF16),
            pltpu.VMEM((3, 288, W), F32),
            pltpu.VMEM((3, 288, W), F32),
            pltpu.VMEM((3, 64, W), F32),
            pltpu.VMEM((544, W), BF16),
            pltpu.VMEM((512, C, TL), F32),
            pltpu.VMEM((2, 32, W), BF16),
            pltpu.VMEM((2, 32, W), BF16),
            pltpu.VMEM((2, CAP * C, TL), F32),
            pltpu.VMEM((PEERS, C, CAP, TL), BF16),
            pltpu.VMEM((PEERS, C, CAP, TL), BF16),
            pltpu.VMEM((PEERS, 1, TL), F32),
            pltpu.VMEM((PEERS // GROUP, AR_DEV, 256), BF16),
            pltpu.VMEM((C * AR_DEV, TL), F32),
            pltpu.VMEM((AR_DEV, TL), F32),
            pltpu.VMEM((C * TL, 256), BF16),
            pltpu.VMEM((2, TL, TL), BF16),
            pltpu.VMEM((2, TL, TL), BF16),
            pltpu.VMEM((4, 16, TL), BF16),
            pltpu.VMEM((2, C, TL), BF16),
            dma((2,)), dma((2,)), dma, dma((PEERS // GROUP,)), dma, dma, dma((8,)), dma((8,)),
        ],
        compiler_params=pltpu.CompilerParams(
            collective_id=0, has_side_effects=True, vmem_limit_bytes=62 * 1024 * 1024
        ),
        cost_estimate=pl.CostEstimate(flops=2 * 10**10, bytes_accessed=3 * 10**7, transcendentals=10**6),
    )(image.reshape(C, ROWS, W), conv_first, conv_second, code, scale_rows, tiles)

    full = lambda shape: pl.BlockSpec(shape, lambda i: (0,) * len(shape))
    return pl.pallas_call(
        uv_kernel,
        out_shape=jax.ShapeDtypeStruct((C, AR_DEV, TL), BF16),
        grid=(AR_DEV // TL,),
        in_specs=[
            full((C, 9 * C)),
            pl.BlockSpec((C, TL, TL), lambda i: (0, i, 0)),
            full((65, C, TL)),
            full((65, C, TL)),
            full((2, TL, TL)),
            full((4, 16, TL)),
        ],
        out_specs=pl.BlockSpec((C, TL, TL), lambda i: (0, i, 0)),
        scratch_shapes=[pltpu.VMEM((768, 288), BF16), pltpu.VMEM((2, TL, TL), F32)],
        compiler_params=pltpu.CompilerParams(vmem_limit_bytes=62 * 1024 * 1024),
        cost_estimate=pl.CostEstimate(flops=10**10, bytes_accessed=10**7, transcendentals=0),
    )(conv_uv, joined, above, below, side_cols, corners)


def solution(mesh):
    return jax.shard_map(
        local,
        mesh=mesh,
        in_specs=(
            P("cam", None, "row", None),
            P(),
            P(),
            P(),
            P("cam", "row", None, None),
            P("cam", "row", None, None),
            P("cam", "row", None, None),
            P("cam", "row", None),
            P("row", "cam", None, None),
        ),
        out_specs=P(None, "row", "cam"),
        check_vma=False,
    )
```

```python
import functools

import jax
import jax.numpy as jnp
from jax import lax
from jax.experimental import pallas as pl
from jax.experimental.pallas import tpu as pltpu
from jax.sharding import PartitionSpec as P

C = 16
W = 2048
TL = 128
CAP = 16
AR_DEV = 1024
PEERS = 128
GROUP = 16
ROWS = 32
F32 = jnp.float32
BF16 = jnp.bfloat16
MESH = pl.DeviceIdType.MESH
NT = (((1,), (1,)), ((), ()))


def iota(shape, dim):
    return lax.broadcasted_iota(jnp.int32, shape, dim)


def dot(a, b):
    return jnp.dot(a, b, preferred_element_type=F32)


def band(weight, m, k, out_of_m, in_of_k):
    pick = jnp.where(out_of_m(iota((m, C), 0))[0] == iota((m, C), 1), 1.0, 0.0).astype(BF16)
    rows = dot(pick, weight).astype(BF16)
    step = in_of_k(iota((m, k), 1))[1] - out_of_m(iota((m, k), 0))[1] + 1
    channel = in_of_k(iota((9 * C, k), 1))[0]
    source = iota((9 * C, k), 0)
    taps = []
    for b in range(3):
        total = jnp.zeros((m, k), F32)
        for a in range(3):
            spread = jnp.where(source == (3 * a + b) * C + channel, 1.0, 0.0).astype(BF16)
            total = total + jnp.where(step == a, dot(rows, spread), 0.0)
        taps.append(total.astype(BF16))
    return taps


def row_major(first):
    return lambda i: (i % C, i // C + first)


def channel_major(first):
    return lambda i: (i // 16, i % 16 + first)


def shift_add(left, mid, right):
    n = mid.shape[1]
    lane = iota(mid.shape, 1)
    a = jnp.where(lane == 0, 0.0, pltpu.roll(left, 1, 1))
    b = jnp.where(lane == n - 1, 0.0, pltpu.roll(right, n - 1, 1))
    return mid + a + b


def join_kernel(
    image, w1, w2, wuv, code, scale_rows, tiles,
    texture,
    joined, above, below, band_uv, side_mats, spread_mat, side_parts, col_sum,
    band1, band1h, band2, part_a, part_b, part_g, hidden, feats,
    edge_out, edge_in, turned, outbox, inbox, scale_in, onehot, total, wsum, pick_cols, cols, side_in, col_in, row_in,
    edge_send, edge_recv, send_sem, recv_sem, ssend_sem, srecv_sem, hsend, hrecv, out_sem,
):
    cam = lax.axis_index("cam")
    row = lax.axis_index("row")
    cams = lax.axis_size("cam")
    strips = lax.axis_size("row")
    me = cam * strips + row

    barrier = pltpu.get_barrier_semaphore()

    def greet(i, carry):
        p = lax.rem(me + i, PEERS)
        pl.semaphore_signal(barrier, inc=1, device_id=(p // strips, p % strips), device_id_type=MESH)
        return carry

    lax.fori_loop(1, PEERS, greet, 0)

    def edges(n, carry):
        at = pl.ds(pl.multiple_of(n * 256, 256), 256)
        for half in range(2):
            field = image[:, half * 16 : half * 16 + 16, at].reshape(256, 256)
            first = 14 if half == 1 else 0
            m, k = iota((32, 256), 0), iota((32, 256), 1)
            pick = jnp.where(k == (m % C) * 16 + first + m // C, 1.0, 0.0).astype(BF16)
            edge_out[half, :, at] = dot(pick, field).astype(BF16)
        return carry

    lax.fori_loop(0, W // 256, edges, 0)
    up = (cam, lax.rem(row + strips - 1, strips))
    down = (cam, lax.rem(row + 1, strips))
    for b, taps in enumerate(band(w1[...], 288, 256, row_major(-1), channel_major(0))):
        band1[b] = taps
    for b, taps in enumerate(band(w1[...], 32, 32, row_major(-1), row_major(-2))):
        band1h[0, b] = taps
    for b, taps in enumerate(band(w1[...], 32, 32, row_major(31), row_major(32))):
        band1h[1, b] = taps
    for b, taps in enumerate(band(w2[...], 224, 256, row_major(0), row_major(-1))):
        band2[b] = taps

    def first_main(n, carry):
        at = pl.ds(pl.multiple_of(n * 256, 256), 256)
        for half, part in ((0, part_a), (1, part_b)):
            field = image[:, half * 16 : half * 16 + 16, at].reshape(256, 256)
            for b in range(3):
                part[b, :, at] = dot(band1[b], field)
        return carry

    lax.fori_loop(0, W // 256, first_main, 0)
    pl.semaphore_wait(barrier, PEERS - 1)
    edge_copies = [
        pltpu.make_async_remote_copy(
            src_ref=edge_out.at[half], dst_ref=edge_in.at[half], send_sem=edge_send.at[half], recv_sem=edge_recv.at[half],
            device_id=where, device_id_type=MESH,
        )
        for half, where in ((0, up), (1, down))
    ]
    for copy in edge_copies:
        copy.start()


    def silu(v):
        return v / (1.0 + jnp.exp(-v))

    def hide(at, sources):
        taps = []
        for b in range(3):
            value = None
            for part, first in sources:
                term = part[b, pl.ds(first, 16), :]
                value = term if value is None else value + term
            taps.append(value)
        return silu(shift_add(*taps))

    def put(at, value):
        hidden[pl.ds(at, 16), :] = value.astype(BF16)

    def body_a(i, carry):
        at = pl.multiple_of(i * 16, 16)
        put(at, hide(i, [(part_a, at)]))
        return carry

    def body_b(i, carry):
        at = pl.multiple_of(i * 16, 16)
        put(at, hide(i, [(part_b, pl.multiple_of(at - 256, 16))]))
        return carry

    lax.fori_loop(2, 16, body_a, 0)
    for i in (16, 17):
        put(i * 16, hide(i, [(part_a, i * 16), (part_b, i * 16 - 256)]))
    lax.fori_loop(18, 32, body_b, 0)

    for copy in edge_copies:
        copy.wait()
    has_above = (row > 0).astype(F32)
    has_below = (row < strips - 1).astype(F32)
    above_bf = has_above.astype(BF16)
    below_bf = has_below.astype(BF16)

    def first_edge(n, carry):
        at = pl.ds(pl.multiple_of(n * 256, 256), 256)
        top = edge_in[1, :, at] * above_bf
        bottom = edge_in[0, :, at] * below_bf
        for b in range(3):
            part_g[b, 0:32, at] = dot(band1h[0, b], top)
            part_g[b, 32:64, at] = dot(band1h[1, b], bottom)
        return carry

    lax.fori_loop(0, W // 256, first_edge, 0)
    put(0, hide(0, [(part_a, 0), (part_g, 0)]) * has_above)
    put(16, hide(1, [(part_a, 16), (part_g, 16)]))
    put(512, hide(32, [(part_b, 256), (part_g, 32)]))
    put(528, hide(33, [(part_b, 272), (part_g, 48)]) * has_below)

    def second(n, carry):
        at = pl.ds(pl.multiple_of(n * 256, 256), 256)
        for b in range(3):
            part_a[b, 0:224, at] = dot(band2[b], hidden[0:256, at])
            part_b[b, 0:224, at] = dot(band2[b], hidden[224:480, at])
            part_g[b, :, at] = dot(band2[b, 0:64, 0:96], hidden[448:544, at])
        return carry

    lax.fori_loop(0, W // 256, second, 0)

    def feature_row(part, first):
        def body(i, carry):
            at = pl.ds(pl.multiple_of(i * 16, 16), 16)
            value = shift_add(part[0, at, :], part[1, at, :], part[2, at, :]).astype(BF16).astype(F32)
            for t in range(W // TL):
                feats[(first + i) * (W // TL) + t] = value[:, t * TL : (t + 1) * TL]
            return carry

        return body

    lax.fori_loop(0, 14, feature_row(part_a, 0), 0)
    lax.fori_loop(0, 14, feature_row(part_b, 14), 0)
    lax.fori_loop(0, 4, feature_row(part_g, 28), 0)

    my, mx, mc = cam // 8, lax.rem(cam // 2, 4), lax.rem(cam, 2)

    def offset(t):
        i, c, b = t % 4, (t // 8) % 4, t // 32

        def order(v):
            w = lax.rem(v, 4)
            return lax.rem(2 * w, 3) + 3 * (w // 3)

        return order(i + b), order(i), (t // 4) % 2, order(i + c)

    def moved(core, sign, t):
        dy, dx, _, dz = offset(t)
        place = (lax.rem(my + 4 + sign * dy, 4) * 4 + lax.rem(mx + 4 + sign * dx, 4)) * 2 + core
        return place * 4 + lax.rem(row + 4 + sign * dz, 4)

    def peer_of(t):
        return moved(lax.rem(mc + offset(t)[2], 2), 1 - 2 * mc, t)

    def source_of(t):
        core = lax.rem(mc + offset(t)[2], 2)
        return moved(core, 2 * core - 1, t)

    def make(p, slot, put_tile):
        for e in range(CAP):
            word = code[p * CAP + e]
            block = word & 511
            shift = (word >> 9) & 127
            scale = (word >> 16).astype(F32) * 0.0625
            turned[slot, e * C : (e + 1) * C, :] = pltpu.roll(feats[block], shift, 1) * scale
        for q in range(C):
            put_tile(q, turned[slot, pl.ds(q, CAP, stride=C), :].astype(BF16))

    def put_own(q, value):
        inbox[0, q] = value

    make(me, 0, put_own)
    scale_in[0] = scale_rows[me]

    def block_copy(t, p):
        return pltpu.make_async_remote_copy(
            src_ref=outbox.at[t], dst_ref=inbox.at[t], send_sem=send_sem,
            recv_sem=recv_sem.at[t // GROUP], device_id=(p // strips, p % strips), device_id_type=MESH,
        )

    def scale_copy(t, p):
        return pltpu.make_async_remote_copy(
            src_ref=scale_rows.at[p], dst_ref=scale_in.at[t], send_sem=ssend_sem, recv_sem=srecv_sem,
            device_id=(p // strips, p % strips), device_id_type=MESH,
        )

    def send_step(t, carry):
        p = peer_of(t)

        def put_tile(q, value):
            outbox[t, q] = value

        make(p, lax.rem(t, 2), put_tile)

        scale_copy(t, p).start()
        block_copy(t, p).start()
        return carry

    lax.fori_loop(1, PEERS, send_step, 0)

    def pick_body(q, carry):
        j, lane = iota((TL, 256), 0), iota((TL, 256), 1)
        hit = ((j == 0) & (lane == q)) | ((j == TL - 1) & (lane == q + TL))
        pick_cols[pl.ds(pl.multiple_of(q * TL, TL), TL), :] = jnp.where(hit, 1.0, 0.0).astype(BF16)
        return carry

    lax.fori_loop(0, C, pick_body, 0)

    def clear(i, carry):
        total[pl.ds(pl.multiple_of(i * 1024, 1024), 1024), :] = jnp.zeros((1024, TL), F32)
        return carry

    lax.fori_loop(0, C, clear, 0)
    wsum[...] = jnp.zeros_like(wsum)
    col_sum[...] = jnp.zeros_like(col_sum)

    def uv_in(i):
        late = i - 256
        return (
            jnp.where(i < 256, i // 16, late % C),
            jnp.where(i < 256, i % 16, jnp.where(late < C, -1, 16)),
        )

    for b, taps in enumerate(band(wuv[...], 256, 288, channel_major(0), uv_in)):
        band_uv[b * 256 : (b + 1) * 256, :] = taps

    lane = iota((TL, TL), 1)
    sub = iota((TL, TL), 0)
    pick = jnp.where(iota((TL, C), 0) % C == iota((TL, C), 1), 1.0, 0.0).astype(BF16)
    uv_rows = dot(pick, wuv[...]).astype(BF16)
    for side in range(2):
        for a in range(3):
            source = iota((9 * C, TL), 0)
            spread = jnp.where(source == (3 * a + 2 * side) * C + iota((9 * C, TL), 1) % C, 1.0, 0.0).astype(BF16)
            side_mats[side, a] = jnp.where(sub // C == lane // C, dot(uv_rows, spread), 0.0).astype(BF16)

    def spread_body(o, carry):
        hit = (sub < 4 * C) & (sub % C == o) & (lane == jnp.where(sub < 2 * C, 0, TL - 1))
        spread_mat[:, pl.ds(pl.multiple_of(o * TL, TL), TL)] = jnp.where(hit, 1.0, 0.0).astype(BF16)
        return carry

    lax.fori_loop(0, C, spread_body, 0)

    def wait_group(g, count):
        pltpu.make_async_remote_copy(
            src_ref=outbox.at[pl.ds(0, count)], dst_ref=inbox.at[pl.ds(0, count)], send_sem=send_sem,
            recv_sem=recv_sem.at[g], device_id=up, device_id_type=MESH,
        ).wait_recv()

    def lanes_of(ref, g, half):
        first = g * GROUP + half * 8
        lane = iota((1, TL), 1) // CAP
        value = jnp.zeros((1, TL), ref.dtype)
        for i in range(8):
            index = first + i if ref is scale_in else source_of(first + i)
            value = jnp.where(lane == i, ref[index], value)
        return value

    def mark_group(g):
        ids = jnp.concatenate([lanes_of(tiles, g, 0), lanes_of(tiles, g, 1)], axis=1)
        for m in range(4):
            hot = jnp.where(iota((256, 256), 0) + m * 256 == ids, 1.0, 0.0).astype(BF16)
            onehot[m * 256 : (m + 1) * 256, :] = hot

    def weigh_group(g, carry):
        mark_group(g)
        weights = jnp.concatenate([lanes_of(scale_in, g, 0), lanes_of(scale_in, g, 1)], axis=1)
        weights = jnp.broadcast_to(weights, (TL, 256)).astype(BF16)
        for m in range(4):
            at = slice(m * 256, (m + 1) * 256)
            wsum[at, :] += lax.dot_general(onehot[at, :], weights, NT, preferred_element_type=F32)
        return carry

    def group_sum(g, t, m):
        block = jnp.concatenate(
            [inbox[pl.ds(g * GROUP, GROUP), 2 * t + h].reshape(256, TL) for h in range(2)], axis=1
        )
        return dot(onehot[m * 256 : (m + 1) * 256, :], block)

    def add_columns(g):
        rows = [inbox[pl.ds(g * GROUP, GROUP), q].reshape(256, TL) for q in range(C)]
        picked = dot(jnp.concatenate(rows, axis=1), pick_cols[...]).astype(BF16)
        for m in range(4):
            at = slice(m * 256, (m + 1) * 256)
            col_sum[at, :] += dot(onehot[at, :], picked)

    def add_group(g):
        add_columns(g)

        def channels(t, carry):
            for m in range(4):
                got = group_sum(g, t, m)
                for h in range(2):
                    at = pl.ds(pl.multiple_of((2 * t + h) * AR_DEV + m * 256, 256), 256)
                    total[at, :] += got[:, h * TL : (h + 1) * TL]
            return carry

        lax.fori_loop(0, C // 2, channels, 0)

    mark_group(0)
    wait_group(0, GROUP - 1)
    add_group(0)

    def receive(g, carry):
        mark_group(g)
        wait_group(g, GROUP)
        add_group(g)
        return carry

    last = PEERS // GROUP - 1
    lax.fori_loop(1, last, receive, 0)
    pltpu.make_async_remote_copy(
        src_ref=scale_rows.at[pl.ds(0, PEERS - 1)], dst_ref=scale_in.at[pl.ds(0, PEERS - 1)], send_sem=ssend_sem,
        recv_sem=srecv_sem, device_id=up, device_id_type=MESH,
    ).wait()
    lax.fori_loop(0, PEERS // GROUP, weigh_group, 0)
    wsum[...] = 1.0 / jnp.maximum(wsum[...], 1.0)
    wait_group(last, GROUP)

    add_columns(last)

    def collect(rb, carry):
        at = pl.ds(pl.multiple_of(rb * TL, TL), TL)
        values = [(col_sum[at, side * TL : (side + 1) * TL] * wsum[at, :]).astype(BF16).astype(F32) for side in range(2)]
        return tuple(c + pltpu.roll(v, rb * C, 1) for c, v in zip(carry, values))

    zero = jnp.zeros((TL, TL), F32)
    left, right = lax.fori_loop(0, AR_DEV // TL, collect, (zero, zero))
    cols[0] = left.astype(BF16)
    cols[1] = right.astype(BF16)

    west, east = lax.rem(cam + cams - 1, cams), lax.rem(cam + 1, cams)
    north, south = lax.rem(row + strips - 1, strips), lax.rem(row + 1, strips)
    plan = [
        (cols.at[1], side_in.at[0], (east, row)),
        (cols.at[0], side_in.at[1], (west, row)),
        (cols.at[1, pl.ds(112, 16)], col_in.at[0], (east, south)),
        (cols.at[1, pl.ds(0, 16)], col_in.at[1], (east, north)),
        (cols.at[0, pl.ds(112, 16)], col_in.at[2], (west, south)),
        (cols.at[0, pl.ds(0, 16)], col_in.at[3], (west, north)),
        (above.at[64], row_in.at[0], (cam, south)),
        (below.at[0], row_in.at[1], (cam, north)),
    ]
    copies = [
        pltpu.make_async_remote_copy(
            src_ref=src, dst_ref=dst, send_sem=hsend.at[i], recv_sem=hrecv.at[i], device_id=where, device_id_type=MESH
        )
        for i, (src, dst, where) in enumerate(plan)
    ]
    for copy in copies[:6]:
        copy.start()

    def finish(t, carry):
        for m in range(4):
            got = group_sum(last, t, m)
            for h in range(2):
                at = pl.ds(pl.multiple_of((2 * t + h) * AR_DEV + m * 256, 256), 256)
                value = (total[at, :] + got[:, h * TL : (h + 1) * TL]) * wsum[m * 256 : (m + 1) * 256, :]
                total[at, :] = value
                joined[2 * t + h, m * 256 : (m + 1) * 256, :] = value.astype(BF16)
        return carry

    lax.fori_loop(0, C // 2, finish, 0)

    def ends(g, carry):
        for last in range(2):
            r = g * 16 + 15 * last
            value = total[pl.ds(r, C, stride=AR_DEV), :].astype(BF16)
            if last:
                above[g + 1] = value
            else:
                below[g] = value
        return carry

    lax.fori_loop(0, 64, ends, 0)

    for copy in copies[6:]:
        copy.start()
    for copy in copies[:6]:
        copy.wait()

    has_side = ((cam > 0).astype(F32), (cam < cams - 1).astype(F32))
    for side in range(2):
        own = side_in[side].astype(F32) * has_side[side]
        top = col_in[2 * side].astype(F32)[15:16, :] * (has_side[side] * has_above)
        bottom = col_in[2 * side + 1].astype(F32)[0:1, :] * (has_side[side] * has_below)
        before = jnp.where(lane[0:1] >= TL - C, top, own[TL - 1 : TL, :])
        before = pltpu.roll(jnp.broadcast_to(before, (TL, TL)), C, 1)
        after = jnp.where(lane[0:1] < C, bottom, own[0:1, :])
        after = pltpu.roll(jnp.broadcast_to(after, (TL, TL)), TL - C, 1)
        shifted = (
            jnp.where(sub == 0, before, pltpu.roll(own, 1, 0)),
            own,
            jnp.where(sub == TL - 1, after, pltpu.roll(own, TL - 1, 0)),
        )
        result = jnp.zeros((TL, TL), F32)
        for a in range(3):
            result = result + lax.dot_general(
                shifted[a].astype(BF16), side_mats[side, a], NT, preferred_element_type=F32
            )
        high = result.astype(BF16).astype(F32)
        side_parts[2 * side] = high
        side_parts[2 * side + 1] = result - high

    tile_lane = iota((16, TL), 1)

    def out_copy(rb):
        at = pl.ds(pl.multiple_of(rb * TL, TL), TL)
        return pltpu.make_async_copy(joined.at[:, at, :], texture.at[:, at, :], out_sem.at[rb])

    def uv_block(rb, carry):
        parts = zero
        for k in range(4):
            turned_part = pltpu.roll(side_parts[k], lax.rem(k * C + TL - rb * C, TL), 1)
            parts = jnp.where(lane // C == k, turned_part, parts)
        parts = parts.astype(BF16)
        for n in range(4):
            at = slice(n * 512, (n + 1) * 512)
            part_a[0, 0:TL, at] = dot(parts, spread_mat[:, at])
        for pair in range(4):
            fields = []
            for h in range(2):
                g = pair * 2 + h
                here = pl.ds(pl.multiple_of(rb * TL + g * 16, 16), 16)
                fields.append(
                    jnp.concatenate([joined[:, here, :].reshape(256, TL), above[rb * 8 + g], below[rb * 8 + g + 1]], axis=0)
                )
            taps = dot(band_uv[...], jnp.concatenate(fields, axis=1))
            for h in range(2):
                g = pair * 2 + h
                here = pl.ds(pl.multiple_of(rb * TL + g * 16, 16), 16)
                cut = slice(h * TL, (h + 1) * TL)
                a = pltpu.roll(taps[0:256, cut], 1, 1)
                m = taps[256:512, cut]
                b = pltpu.roll(taps[512:768, cut], TL - 1, 1)
                for o in range(C):
                    rows = slice(o * 16, (o + 1) * 16)
                    low = jnp.where(tile_lane == 0, 0.0, a[rows])
                    high = jnp.where(tile_lane == TL - 1, 0.0, b[rows])
                    side = part_a[0, g * 16 : (g + 1) * 16, o * TL : (o + 1) * TL]
                    value = joined[o, here, :].astype(F32) + side + m[rows] + low + high
                    joined[o, here, :] = value.astype(BF16)
        out_copy(rb).start()
        return carry

    lax.fori_loop(1, 7, uv_block, 0)
    pltpu.make_async_remote_copy(
        src_ref=outbox.at[pl.ds(0, PEERS - 1)], dst_ref=inbox.at[pl.ds(0, PEERS - 1)], send_sem=send_sem,
        recv_sem=recv_sem.at[0], device_id=up, device_id_type=MESH,
    ).wait_send()
    for copy in copies[6:]:
        copy.wait()
    above[0] = row_in[0] * above_bf
    below[64] = row_in[1] * below_bf

    def outer_block(i, carry):
        return uv_block(i * 7, carry)

    lax.fori_loop(0, 2, outer_block, 0)

    def out_wait(rb, carry):
        out_copy(rb).wait()
        return carry

    lax.fori_loop(0, 8, out_wait, 0)


def local(image, conv_first, conv_second, conv_uv, send_block, send_shift, send_weight, send_count, recv_tile):
    block = send_block.reshape(PEERS, CAP)
    shift = send_shift.reshape(PEERS, CAP)
    valid = lax.broadcasted_iota(jnp.int32, (PEERS, CAP), 1) < send_count.reshape(PEERS, 1)
    weight = jnp.where(valid, send_weight.reshape(PEERS, CAP), 0)
    code = (block + shift * 512 + weight * 65536).reshape(PEERS * CAP)
    scale = weight.astype(F32) * 0.0625
    scale_rows = jnp.tile(scale, (1, 8)).reshape(PEERS, 1, TL)
    tiles = jnp.tile(recv_tile.reshape(PEERS, CAP), (1, 8)).reshape(PEERS, 1, TL)

    vmem = pl.BlockSpec(memory_space=pltpu.VMEM)
    smem = pl.BlockSpec(memory_space=pltpu.SMEM)
    dma = pltpu.SemaphoreType.DMA
    return pl.pallas_call(
        join_kernel,
        out_shape=jax.ShapeDtypeStruct((C, AR_DEV, TL), BF16),
        in_specs=[vmem, vmem, vmem, vmem, smem, vmem, vmem],
        out_specs=pl.BlockSpec(memory_space=pl.ANY),
        scratch_shapes=[
            pltpu.VMEM((C, AR_DEV, TL), BF16),
            pltpu.VMEM((65, C, TL), BF16),
            pltpu.VMEM((65, C, TL), BF16),
            pltpu.VMEM((768, 288), BF16),
            pltpu.VMEM((2, 3, TL, TL), BF16),
            pltpu.VMEM((TL, C * TL), BF16),
            pltpu.VMEM((4, TL, TL), F32),
            pltpu.VMEM((AR_DEV, 256), F32),
            pltpu.VMEM((3, 288, 256), BF16),
            pltpu.VMEM((2, 3, 32, 32), BF16),
            pltpu.VMEM((3, 224, 256), BF16),
            pltpu.VMEM((3, 288, W), F32),
            pltpu.VMEM((3, 288, W), F32),
            pltpu.VMEM((3, 64, W), F32),
            pltpu.VMEM((544, W), BF16),
            pltpu.VMEM((512, C, TL), F32),
            pltpu.VMEM((2, 32, W), BF16),
            pltpu.VMEM((2, 32, W), BF16),
            pltpu.VMEM((2, CAP * C, TL), F32),
            pltpu.VMEM((PEERS, C, CAP, TL), BF16),
            pltpu.VMEM((PEERS, C, CAP, TL), BF16),
            pltpu.VMEM((PEERS, 1, TL), F32),
            pltpu.VMEM((AR_DEV, 256), BF16),
            pltpu.VMEM((C * AR_DEV, TL), F32),
            pltpu.VMEM((AR_DEV, TL), F32),
            pltpu.VMEM((C * TL, 256), BF16),
            pltpu.VMEM((2, TL, TL), BF16),
            pltpu.VMEM((2, TL, TL), BF16),
            pltpu.VMEM((4, 16, TL), BF16),
            pltpu.VMEM((2, C, TL), BF16),
            dma((2,)), dma((2,)), dma, dma((PEERS // GROUP,)), dma, dma, dma((8,)), dma((8,)), dma((8,)),
        ],
        compiler_params=pltpu.CompilerParams(
            collective_id=0, has_side_effects=True, vmem_limit_bytes=62 * 1024 * 1024
        ),
        cost_estimate=pl.CostEstimate(flops=2 * 10**10, bytes_accessed=3 * 10**7, transcendentals=10**6),
    )(image.reshape(C, ROWS, W), conv_first, conv_second, conv_uv, code, scale_rows, tiles)


def solution(mesh):
    return jax.shard_map(
        local,
        mesh=mesh,
        in_specs=(
            P("cam", None, "row", None),
            P(),
            P(),
            P(),
            P("cam", "row", None, None),
            P("cam", "row", None, None),
            P("cam", "row", None, None),
            P("cam", "row", None),
            P("row", "cam", None, None),
        ),
        out_specs=P(None, "row", "cam"),
        check_vma=False,
    )
```

```python
import functools

import jax
import jax.numpy as jnp
import numpy as np
from jax import lax
from jax.experimental import pallas as pl
from jax.experimental.pallas import tpu as pltpu
from jax.sharding import PartitionSpec as P

C = 16
W = 2048
TL = 128
CAP = 16
AR_DEV = 1024
PEERS = 128
GROUP = 16
ROWS = 32
F32 = jnp.float32
BF16 = jnp.bfloat16
MESH = pl.DeviceIdType.MESH
NT = (((1,), (1,)), ((), ()))
TN = (((0,), (0,)), ((), ()))


def iota(shape, dim):
    return lax.broadcasted_iota(jnp.int32, shape, dim)


def dot(a, b):
    return jnp.dot(a, b, preferred_element_type=F32)


def band(weight, m, k, out_of_m, in_of_k):
    pick = jnp.where(out_of_m(iota((m, C), 0))[0] == iota((m, C), 1), 1.0, 0.0).astype(BF16)
    rows = dot(pick, weight).astype(BF16)
    step = in_of_k(iota((m, k), 1))[1] - out_of_m(iota((m, k), 0))[1] + 1
    channel = in_of_k(iota((9 * C, k), 1))[0]
    source = iota((9 * C, k), 0)
    taps = []
    for b in range(3):
        total = jnp.zeros((m, k), F32)
        for a in range(3):
            spread = jnp.where(source == (3 * a + b) * C + channel, 1.0, 0.0).astype(BF16)
            total = total + jnp.where(step == a, dot(rows, spread), 0.0)
        taps.append(total.astype(BF16))
    return taps


def row_major(first):
    return lambda i: (i % C, i // C + first)


def channel_major(first):
    return lambda i: (i // 16, i % 16 + first)


def shift_add(left, mid, right):
    n = mid.shape[1]
    lane = iota(mid.shape, 1)
    a = jnp.where(lane == 0, 0.0, pltpu.roll(left, 1, 1))
    b = jnp.where(lane == n - 1, 0.0, pltpu.roll(right, n - 1, 1))
    return mid + a + b


def join_kernel(
    image, w1, w2, wuv, code, code_rows, tile_rows,
    joined_out, above, below, band_uv, side_parts,
    joined, scale_rows, tiles, side_mats, col_sum,
    band1, band1h, band2, part_a, part_b, part_g, hidden, feats,
    edge_out, edge_in, turned, outbox, inbox, scale_in, onehot, total, wsum, pick_cols, cols, side_in, col_in, row_in,
    edge_send, edge_recv, send_sem, recv_sem, ssend_sem, srecv_sem, hsend, hrecv, out_sem,
):
    cam = lax.axis_index("cam")
    row = lax.axis_index("row")
    cams = lax.axis_size("cam")
    strips = lax.axis_size("row")
    me = cam * strips + row

    barrier = pltpu.get_barrier_semaphore()

    def greet(i, carry):
        p = lax.rem(me + i, PEERS)
        pl.semaphore_signal(barrier, inc=1, device_id=(p // strips, p % strips), device_id_type=MESH)
        return carry

    lax.fori_loop(1, PEERS, greet, 0)

    repeat = jnp.where(iota((CAP, TL), 1) % CAP == iota((CAP, TL), 0), 1.0, 0.0).astype(BF16)
    def table(numbers):
        return lax.dot_general(numbers.astype(F32).astype(BF16), repeat, TN, preferred_element_type=F32)

    scale_table = table(code_rows[...] >> 16) * 0.0625
    tile_table = table(tile_rows[...] >> 5) * 32.0 + table(tile_rows[...] & 31)
    for i in range(PEERS // 8):
        at = slice(i * 8, i * 8 + 8)
        scale_rows[at] = scale_table[at].reshape(8, 1, TL)
        tiles[at] = tile_table[at].reshape(8, 1, TL)

    def edges(n, carry):
        at = pl.ds(pl.multiple_of(n * 256, 256), 256)
        for half in range(2):
            field = image[:, half * 16 : half * 16 + 16, at].reshape(256, 256)
            first = 14 if half == 1 else 0
            m, k = iota((32, 256), 0), iota((32, 256), 1)
            pick = jnp.where(k == (m % C) * 16 + first + m // C, 1.0, 0.0).astype(BF16)
            edge_out[half, :, at] = dot(pick, field).astype(BF16)
        return carry

    lax.fori_loop(0, W // 256, edges, 0)
    up = (cam, lax.rem(row + strips - 1, strips))
    down = (cam, lax.rem(row + 1, strips))
    for b, taps in enumerate(band(w1[...], 288, 256, row_major(-1), channel_major(0))):
        band1[b] = taps
    for b, taps in enumerate(band(w1[...], 32, 32, row_major(-1), row_major(-2))):
        band1h[0, b] = taps
    for b, taps in enumerate(band(w1[...], 32, 32, row_major(31), row_major(32))):
        band1h[1, b] = taps
    for b, taps in enumerate(band(w2[...], 224, 256, row_major(0), row_major(-1))):
        band2[b] = taps

    def first_main(n, carry):
        at = pl.ds(pl.multiple_of(n * 256, 256), 256)
        for half, part in ((0, part_a), (1, part_b)):
            field = image[:, half * 16 : half * 16 + 16, at].reshape(256, 256)
            for b in range(3):
                part[b, :, at] = dot(band1[b], field)
        return carry

    lax.fori_loop(0, W // 256, first_main, 0)
    pl.semaphore_wait(barrier, PEERS - 1)
    edge_copies = [
        pltpu.make_async_remote_copy(
            src_ref=edge_out.at[half], dst_ref=edge_in.at[half], send_sem=edge_send.at[half], recv_sem=edge_recv.at[half],
            device_id=where, device_id_type=MESH,
        )
        for half, where in ((0, up), (1, down))
    ]
    for copy in edge_copies:
        copy.start()


    def silu(v):
        return v / (1.0 + jnp.exp(-v))

    def hide(at, sources):
        taps = []
        for b in range(3):
            value = None
            for part, first in sources:
                term = part[b, pl.ds(first, 16), :]
                value = term if value is None else value + term
            taps.append(value)
        return silu(shift_add(*taps))

    def put(at, value):
        hidden[pl.ds(at, 16), :] = value.astype(BF16)

    def body_a(i, carry):
        at = pl.multiple_of(i * 16, 16)
        put(at, hide(i, [(part_a, at)]))
        return carry

    def body_b(i, carry):
        at = pl.multiple_of(i * 16, 16)
        put(at, hide(i, [(part_b, pl.multiple_of(at - 256, 16))]))
        return carry

    lax.fori_loop(2, 16, body_a, 0)
    for i in (16, 17):
        put(i * 16, hide(i, [(part_a, i * 16), (part_b, i * 16 - 256)]))
    lax.fori_loop(18, 32, body_b, 0)

    for copy in edge_copies:
        copy.wait()
    has_above = (row > 0).astype(F32)
    has_below = (row < strips - 1).astype(F32)
    above_bf = has_above.astype(BF16)
    below_bf = has_below.astype(BF16)

    def first_edge(n, carry):
        at = pl.ds(pl.multiple_of(n * 256, 256), 256)
        top = edge_in[1, :, at] * above_bf
        bottom = edge_in[0, :, at] * below_bf
        for b in range(3):
            part_g[b, 0:32, at] = dot(band1h[0, b], top)
            part_g[b, 32:64, at] = dot(band1h[1, b], bottom)
        return carry

    lax.fori_loop(0, W // 256, first_edge, 0)
    put(0, hide(0, [(part_a, 0), (part_g, 0)]) * has_above)
    put(16, hide(1, [(part_a, 16), (part_g, 16)]))
    put(512, hide(32, [(part_b, 256), (part_g, 32)]))
    put(528, hide(33, [(part_b, 272), (part_g, 48)]) * has_below)

    def second(n, carry):
        at = pl.ds(pl.multiple_of(n * 256, 256), 256)
        for b in range(3):
            part_a[b, 0:224, at] = dot(band2[b], hidden[0:256, at])
            part_b[b, 0:224, at] = dot(band2[b], hidden[224:480, at])
            part_g[b, :, at] = dot(band2[b, 0:64, 0:96], hidden[448:544, at])
        return carry

    lax.fori_loop(0, W // 256, second, 0)

    def feature_row(part, first):
        def body(i, carry):
            at = pl.ds(pl.multiple_of(i * 16, 16), 16)
            value = shift_add(part[0, at, :], part[1, at, :], part[2, at, :]).astype(BF16).astype(F32)
            for t in range(W // TL):
                feats[(first + i) * (W // TL) + t] = value[:, t * TL : (t + 1) * TL]
            return carry

        return body

    lax.fori_loop(0, 14, feature_row(part_a, 0), 0)
    lax.fori_loop(0, 14, feature_row(part_b, 14), 0)
    lax.fori_loop(0, 4, feature_row(part_g, 28), 0)

    my, mx, mc = cam // 8, lax.rem(cam // 2, 4), lax.rem(cam, 2)

    def offset(t):
        i, c, b = t % 4, (t // 8) % 4, t // 32

        def order(v):
            w = lax.rem(v, 4)
            return lax.rem(2 * w, 3) + 3 * (w // 3)

        return order(i + b), order(i), (t // 4) % 2, order(i + c)

    def moved(core, sign, t):
        dy, dx, _, dz = offset(t)
        place = (lax.rem(my + 4 + sign * dy, 4) * 4 + lax.rem(mx + 4 + sign * dx, 4)) * 2 + core
        return place * 4 + lax.rem(row + 4 + sign * dz, 4)

    def peer_of(t):
        return moved(lax.rem(mc + offset(t)[2], 2), 1 - 2 * mc, t)

    def source_of(t):
        core = lax.rem(mc + offset(t)[2], 2)
        return moved(core, 2 * core - 1, t)

    def make(p, slot, put_tile):
        for e in range(CAP):
            word = code[e, p]
            block = word & 511
            shift = (word >> 9) & 127
            scale = (word >> 16).astype(F32) * 0.0625
            turned[slot, e * C : (e + 1) * C, :] = pltpu.roll(feats[block], shift, 1) * scale
        for q in range(C):
            put_tile(q, turned[slot, pl.ds(q, CAP, stride=C), :].astype(BF16))

    def put_own(q, value):
        inbox[0, q] = value

    make(me, 0, put_own)
    scale_in[0] = scale_rows[me]

    def block_copy(t, p):
        return pltpu.make_async_remote_copy(
            src_ref=outbox.at[t], dst_ref=inbox.at[t], send_sem=send_sem,
            recv_sem=recv_sem.at[t // GROUP], device_id=(p // strips, p % strips), device_id_type=MESH,
        )

    def scale_copy(t, p):
        return pltpu.make_async_remote_copy(
            src_ref=scale_rows.at[p], dst_ref=scale_in.at[t], send_sem=ssend_sem, recv_sem=srecv_sem,
            device_id=(p // strips, p % strips), device_id_type=MESH,
        )

    def send_step(t, carry):
        p = peer_of(t)

        def put_tile(q, value):
            outbox[t, q] = value

        make(p, lax.rem(t, 2), put_tile)

        scale_copy(t, p).start()
        block_copy(t, p).start()
        return carry

    lax.fori_loop(1, PEERS, send_step, 0)

    def pick_body(q, carry):
        j, lane = iota((TL, 256), 0), iota((TL, 256), 1)
        hit = ((j == 0) & (lane == q)) | ((j == TL - 1) & (lane == q + TL))
        pick_cols[pl.ds(pl.multiple_of(q * TL, TL), TL), :] = jnp.where(hit, 1.0, 0.0).astype(BF16)
        return carry

    lax.fori_loop(0, C, pick_body, 0)

    def clear(i, carry):
        total[pl.ds(pl.multiple_of(i * 1024, 1024), 1024), :] = jnp.zeros((1024, TL), F32)
        return carry

    lax.fori_loop(0, C, clear, 0)
    wsum[...] = jnp.zeros_like(wsum)
    col_sum[...] = jnp.zeros_like(col_sum)

    def uv_in(i):
        late = i - 256
        return (
            jnp.where(i < 256, i // 16, late % C),
            jnp.where(i < 256, i % 16, jnp.where(late < C, -1, 16)),
        )

    for b, taps in enumerate(band(wuv[...], 256, 288, channel_major(0), uv_in)):
        band_uv[b * 256 : (b + 1) * 256, :] = taps

    lane = iota((TL, TL), 1)
    sub = iota((TL, TL), 0)
    pick = jnp.where(iota((TL, C), 0) % C == iota((TL, C), 1), 1.0, 0.0).astype(BF16)
    uv_rows = dot(pick, wuv[...]).astype(BF16)
    for side in range(2):
        for a in range(3):
            source = iota((9 * C, TL), 0)
            spread = jnp.where(source == (3 * a + 2 * side) * C + iota((9 * C, TL), 1) % C, 1.0, 0.0).astype(BF16)
            side_mats[side, a] = jnp.where(sub // C == lane // C, dot(uv_rows, spread), 0.0).astype(BF16)

    def wait_group(g, count):
        pltpu.make_async_remote_copy(
            src_ref=outbox.at[pl.ds(0, count)], dst_ref=inbox.at[pl.ds(0, count)], send_sem=send_sem,
            recv_sem=recv_sem.at[g], device_id=up, device_id_type=MESH,
        ).wait_recv()

    def lanes_of(ref, g, half):
        first = g * GROUP + half * 8
        lane = iota((1, TL), 1) // CAP
        value = jnp.zeros((1, TL), ref.dtype)
        for i in range(8):
            index = first + i if ref is scale_in else source_of(first + i)
            value = jnp.where(lane == i, ref[index], value)
        return value

    def mark_group(g):
        ids = jnp.concatenate([lanes_of(tiles, g, 0), lanes_of(tiles, g, 1)], axis=1)
        for m in range(4):
            hot = jnp.where((iota((256, 256), 0) + m * 256).astype(F32) == ids, 1.0, 0.0).astype(BF16)
            onehot[m * 256 : (m + 1) * 256, :] = hot

    def weigh_group(g, carry):
        mark_group(g)
        weights = jnp.concatenate([lanes_of(scale_in, g, 0), lanes_of(scale_in, g, 1)], axis=1)
        weights = jnp.broadcast_to(weights, (TL, 256)).astype(BF16)
        for m in range(4):
            at = slice(m * 256, (m + 1) * 256)
            wsum[at, :] += lax.dot_general(onehot[at, :], weights, NT, preferred_element_type=F32)
        return carry

    def group_sum(g, t, m):
        block = jnp.concatenate(
            [inbox[pl.ds(g * GROUP, GROUP), 2 * t + h].reshape(256, TL) for h in range(2)], axis=1
        )
        return dot(onehot[m * 256 : (m + 1) * 256, :], block)

    def add_columns(g):
        rows = [inbox[pl.ds(g * GROUP, GROUP), q].reshape(256, TL) for q in range(C)]
        picked = dot(jnp.concatenate(rows, axis=1), pick_cols[...]).astype(BF16)
        for m in range(4):
            at = slice(m * 256, (m + 1) * 256)
            col_sum[at, :] += dot(onehot[at, :], picked)

    def add_group(g):
        add_columns(g)

        def channels(t, carry):
            for m in range(4):
                got = group_sum(g, t, m)
                for h in range(2):
                    at = pl.ds(pl.multiple_of((2 * t + h) * AR_DEV + m * 256, 256), 256)
                    total[at, :] += got[:, h * TL : (h + 1) * TL]
            return carry

        lax.fori_loop(0, C // 2, channels, 0)

    mark_group(0)
    wait_group(0, GROUP - 1)
    add_group(0)

    def receive(g, carry):
        mark_group(g)
        wait_group(g, GROUP)
        add_group(g)
        return carry

    last = PEERS // GROUP - 1
    lax.fori_loop(1, last, receive, 0)
    pltpu.make_async_remote_copy(
        src_ref=scale_rows.at[pl.ds(0, PEERS - 1)], dst_ref=scale_in.at[pl.ds(0, PEERS - 1)], send_sem=ssend_sem,
        recv_sem=srecv_sem, device_id=up, device_id_type=MESH,
    ).wait()
    lax.fori_loop(0, PEERS // GROUP, weigh_group, 0)
    wsum[...] = 1.0 / jnp.maximum(wsum[...], 1.0)
    wait_group(last, GROUP)

    add_columns(last)

    def collect(rb, carry):
        at = pl.ds(pl.multiple_of(rb * TL, TL), TL)
        values = [(col_sum[at, side * TL : (side + 1) * TL] * wsum[at, :]).astype(BF16).astype(F32) for side in range(2)]
        return tuple(c + pltpu.roll(v, rb * C, 1) for c, v in zip(carry, values))

    zero = jnp.zeros((TL, TL), F32)
    left, right = lax.fori_loop(0, AR_DEV // TL, collect, (zero, zero))
    cols[0] = left.astype(BF16)
    cols[1] = right.astype(BF16)

    west, east = lax.rem(cam + cams - 1, cams), lax.rem(cam + 1, cams)
    north, south = lax.rem(row + strips - 1, strips), lax.rem(row + 1, strips)
    plan = [
        (cols.at[1], side_in.at[0], (east, row)),
        (cols.at[0], side_in.at[1], (west, row)),
        (cols.at[1, pl.ds(112, 16)], col_in.at[0], (east, south)),
        (cols.at[1, pl.ds(0, 16)], col_in.at[1], (east, north)),
        (cols.at[0, pl.ds(112, 16)], col_in.at[2], (west, south)),
        (cols.at[0, pl.ds(0, 16)], col_in.at[3], (west, north)),
        (above.at[64], row_in.at[0], (cam, south)),
        (below.at[0], row_in.at[1], (cam, north)),
    ]
    copies = [
        pltpu.make_async_remote_copy(
            src_ref=src, dst_ref=dst, send_sem=hsend.at[i], recv_sem=hrecv.at[i], device_id=where, device_id_type=MESH
        )
        for i, (src, dst, where) in enumerate(plan)
    ]
    for copy in copies[:6]:
        copy.start()

    def out_copy(t):
        at = pl.ds(2 * t, 2)
        return pltpu.make_async_copy(joined.at[at], joined_out.at[at], out_sem.at[t])

    def finish(t, carry):
        for m in range(4):
            got = group_sum(last, t, m)
            for h in range(2):
                at = pl.ds(pl.multiple_of((2 * t + h) * AR_DEV + m * 256, 256), 256)
                value = (total[at, :] + got[:, h * TL : (h + 1) * TL]) * wsum[m * 256 : (m + 1) * 256, :]
                total[at, :] = value
                joined[2 * t + h, m * 256 : (m + 1) * 256, :] = value.astype(BF16)
        out_copy(t).start()
        return carry

    lax.fori_loop(0, C // 2, finish, 0)

    def ends(g, carry):
        for last in range(2):
            r = g * 16 + 15 * last
            value = total[pl.ds(r, C, stride=AR_DEV), :].astype(BF16)
            if last:
                above[g + 1] = value
            else:
                below[g] = value
        return carry

    lax.fori_loop(0, 64, ends, 0)

    for copy in copies[6:]:
        copy.start()
    for copy in copies[:6]:
        copy.wait()

    has_side = ((cam > 0).astype(F32), (cam < cams - 1).astype(F32))
    for side in range(2):
        own = side_in[side].astype(F32) * has_side[side]
        top = col_in[2 * side].astype(F32)[15:16, :] * (has_side[side] * has_above)
        bottom = col_in[2 * side + 1].astype(F32)[0:1, :] * (has_side[side] * has_below)
        before = jnp.where(lane[0:1] >= TL - C, top, own[TL - 1 : TL, :])
        before = pltpu.roll(jnp.broadcast_to(before, (TL, TL)), C, 1)
        after = jnp.where(lane[0:1] < C, bottom, own[0:1, :])
        after = pltpu.roll(jnp.broadcast_to(after, (TL, TL)), TL - C, 1)
        shifted = (
            jnp.where(sub == 0, before, pltpu.roll(own, 1, 0)),
            own,
            jnp.where(sub == TL - 1, after, pltpu.roll(own, TL - 1, 0)),
        )
        result = jnp.zeros((TL, TL), F32)
        for a in range(3):
            result = result + lax.dot_general(
                shifted[a].astype(BF16), side_mats[side, a], NT, preferred_element_type=F32
            )
        high = result.astype(BF16)
        side_parts[2 * side] = high
        side_parts[2 * side + 1] = (result - high.astype(F32)).astype(BF16)

    pltpu.make_async_remote_copy(
        src_ref=outbox.at[pl.ds(0, PEERS - 1)], dst_ref=inbox.at[pl.ds(0, PEERS - 1)], send_sem=send_sem,
        recv_sem=recv_sem.at[0], device_id=up, device_id_type=MESH,
    ).wait_send()
    for copy in copies[6:]:
        copy.wait()
    above[0] = row_in[0] * above_bf
    below[64] = row_in[1] * below_bf

    def out_wait(t, carry):
        out_copy(t).wait()
        return carry

    lax.fori_loop(0, C // 2, out_wait, 0)


def uv_kernel(joined, above, below, bands, side_parts, spread_mat, texture, side_plane):
    rb = pl.program_id(0)
    lane = iota((TL, TL), 1)
    parts = jnp.zeros((TL, TL), F32)
    for k in range(4):
        turned = pltpu.roll(side_parts[k].astype(F32), lax.rem(k * C + TL - rb * C, TL), 1)
        parts = jnp.where(lane // C == k, turned, parts)
    parts = parts.astype(BF16)
    for n in range(4):
        at = slice(n * 512, (n + 1) * 512)
        side_plane[:, at] = dot(parts, spread_mat[:, at])
    tile_lane = iota((16, TL), 1)
    for pair in range(4):
        fields = []
        for h in range(2):
            g = pair * 2 + h
            here = slice(g * 16, (g + 1) * 16)
            fields.append(
                jnp.concatenate([joined[:, here, :].reshape(256, TL), above[rb * 8 + g], below[rb * 8 + g + 1]], axis=0)
            )
        taps = dot(bands[...], jnp.concatenate(fields, axis=1))
        for h in range(2):
            g = pair * 2 + h
            here = slice(g * 16, (g + 1) * 16)
            cut = slice(h * TL, (h + 1) * TL)
            a = pltpu.roll(taps[0:256, cut], 1, 1)
            m = taps[256:512, cut]
            b = pltpu.roll(taps[512:768, cut], TL - 1, 1)
            for o in range(C):
                rows = slice(o * 16, (o + 1) * 16)
                low = jnp.where(tile_lane == 0, 0.0, a[rows])
                high = jnp.where(tile_lane == TL - 1, 0.0, b[rows])
                side = side_plane[here, o * TL : (o + 1) * TL]
                value = joined[o, here, :].astype(F32) + side + m[rows] + low + high
                texture[o, here, :] = value.astype(BF16)


def local(image, conv_first, conv_second, conv_uv, send_block, send_shift, send_weight, send_count, recv_tile):
    valid = lax.broadcasted_iota(jnp.int32, (CAP, PEERS), 0) < send_count.reshape(1, PEERS)
    weight = jnp.where(valid, send_weight.reshape(PEERS, CAP).T, 0)
    code = send_block.reshape(PEERS, CAP).T + send_shift.reshape(PEERS, CAP).T * 512 + weight * 65536
    tile_rows = recv_tile.reshape(PEERS, CAP).T

    vmem = pl.BlockSpec(memory_space=pltpu.VMEM)
    smem = pl.BlockSpec(memory_space=pltpu.SMEM)
    dma = pltpu.SemaphoreType.DMA
    joined, above, below, bands, side_parts = pl.pallas_call(
        join_kernel,
        out_shape=[
            jax.ShapeDtypeStruct((C, AR_DEV, TL), BF16),
            jax.ShapeDtypeStruct((65, C, TL), BF16),
            jax.ShapeDtypeStruct((65, C, TL), BF16),
            jax.ShapeDtypeStruct((768, 288), BF16),
            jax.ShapeDtypeStruct((4, TL, TL), BF16),
        ],
        in_specs=[vmem, vmem, vmem, vmem, smem, vmem, vmem],
        out_specs=[pl.BlockSpec(memory_space=pl.ANY)] + [vmem] * 4,
        scratch_shapes=[
            pltpu.VMEM((C, AR_DEV, TL), BF16),
            pltpu.VMEM((PEERS, 1, TL), F32),
            pltpu.VMEM((PEERS, 1, TL), F32),
            pltpu.VMEM((2, 3, TL, TL), BF16),
            pltpu.VMEM((AR_DEV, 256), F32),
            pltpu.VMEM((3, 288, 256), BF16),
            pltpu.VMEM((2, 3, 32, 32), BF16),
            pltpu.VMEM((3, 224, 256), BF16),
            pltpu.VMEM((3, 288, W), F32),
            pltpu.VMEM((3, 288, W), F32),
            pltpu.VMEM((3, 64, W), F32),
            pltpu.VMEM((544, W), BF16),
            pltpu.VMEM((512, C, TL), F32),
            pltpu.VMEM((2, 32, W), BF16),
            pltpu.VMEM((2, 32, W), BF16),
            pltpu.VMEM((2, CAP * C, TL), F32),
            pltpu.VMEM((PEERS, C, CAP, TL), BF16),
            pltpu.VMEM((PEERS, C, CAP, TL), BF16),
            pltpu.VMEM((PEERS, 1, TL), F32),
            pltpu.VMEM((AR_DEV, 256), BF16),
            pltpu.VMEM((C * AR_DEV, TL), F32),
            pltpu.VMEM((AR_DEV, TL), F32),
            pltpu.VMEM((C * TL, 256), BF16),
            pltpu.VMEM((2, TL, TL), BF16),
            pltpu.VMEM((2, TL, TL), BF16),
            pltpu.VMEM((4, 16, TL), BF16),
            pltpu.VMEM((2, C, TL), BF16),
            dma((2,)), dma((2,)), dma, dma((PEERS // GROUP,)), dma, dma, dma((8,)), dma((8,)), dma((8,)),
        ],
        compiler_params=pltpu.CompilerParams(
            collective_id=0, has_side_effects=True, vmem_limit_bytes=62 * 1024 * 1024
        ),
        cost_estimate=pl.CostEstimate(flops=2 * 10**10, bytes_accessed=3 * 10**7, transcendentals=10**6),
    )(image.reshape(C, ROWS, W), conv_first, conv_second, conv_uv, code, code, tile_rows)

    k, o = np.arange(TL)[:, None, None] // C, np.arange(TL)[:, None, None] % C
    channel, column = np.arange(C)[None, :, None], np.arange(TL)[None, None, :]
    spread = ((k < 4) & (o == channel) & (column == np.where(k < 2, 0, TL - 1))).reshape(TL, C * TL)
    full = lambda shape: pl.BlockSpec(shape, lambda i: (0,) * len(shape))
    return pl.pallas_call(
        uv_kernel,
        out_shape=jax.ShapeDtypeStruct((C, AR_DEV, TL), BF16),
        grid=(AR_DEV // TL,),
        in_specs=[
            pl.BlockSpec((C, TL, TL), lambda i: (0, i, 0)),
            full((65, C, TL)),
            full((65, C, TL)),
            full((768, 288)),
            full((4, TL, TL)),
            full((TL, C * TL)),
        ],
        out_specs=pl.BlockSpec((C, TL, TL), lambda i: (0, i, 0)),
        scratch_shapes=[pltpu.VMEM((TL, C * TL), F32)],
        compiler_params=pltpu.CompilerParams(vmem_limit_bytes=62 * 1024 * 1024),
        cost_estimate=pl.CostEstimate(flops=10**10, bytes_accessed=10**7, transcendentals=0),
    )(joined, above, below, bands, side_parts, jnp.asarray(spread.astype(np.float32)).astype(BF16))


def solution(mesh):
    return jax.shard_map(
        local,
        mesh=mesh,
        in_specs=(
            P("cam", None, "row", None),
            P(),
            P(),
            P(),
            P("cam", "row", None, None),
            P("cam", "row", None, None),
            P("cam", "row", None, None),
            P("cam", "row", None),
            P("row", "cam", None, None),
        ),
        out_specs=P(None, "row", "cam"),
        check_vma=False,
    )
```

```python
import functools

import jax
import jax.numpy as jnp
import numpy as np
from jax import lax
from jax.experimental import pallas as pl
from jax.experimental.pallas import tpu as pltpu
from jax.sharding import PartitionSpec as P

C = 16
W = 2048
TL = 128
CAP = 16
AR_DEV = 1024
PEERS = 128
GROUP = 16
ROWS = 32
F32 = jnp.float32
BF16 = jnp.bfloat16
MESH = pl.DeviceIdType.MESH
NT = (((1,), (1,)), ((), ()))
TN = (((0,), (0,)), ((), ()))


def iota(shape, dim):
    return lax.broadcasted_iota(jnp.int32, shape, dim)


def dot(a, b):
    return jnp.dot(a, b, preferred_element_type=F32)


def band(weight, m, k, out_of_m, in_of_k):
    pick = jnp.where(out_of_m(iota((m, C), 0))[0] == iota((m, C), 1), 1.0, 0.0).astype(BF16)
    rows = dot(pick, weight).astype(BF16)
    step = in_of_k(iota((m, k), 1))[1] - out_of_m(iota((m, k), 0))[1] + 1
    channel = in_of_k(iota((9 * C, k), 1))[0]
    source = iota((9 * C, k), 0)
    taps = []
    for b in range(3):
        total = jnp.zeros((m, k), F32)
        for a in range(3):
            spread = jnp.where(source == (3 * a + b) * C + channel, 1.0, 0.0).astype(BF16)
            total = total + jnp.where(step == a, dot(rows, spread), 0.0)
        taps.append(total.astype(BF16))
    return taps


def row_major(first):
    return lambda i: (i % C, i // C + first)


def channel_major(first):
    return lambda i: (i // 16, i % 16 + first)


def shift_add(left, mid, right):
    n = mid.shape[1]
    lane = iota(mid.shape, 1)
    a = jnp.where(lane == 0, 0.0, pltpu.roll(left, 1, 1))
    b = jnp.where(lane == n - 1, 0.0, pltpu.roll(right, n - 1, 1))
    return mid + a + b


def join_kernel(
    image, w1, w2, wuv, code, code_rows, tile_rows,
    joined_out, above, below, band_uv, side_parts,
    joined, scale_rows, tiles, side_mats, col_sum,
    band1, band1h, band2, part_a, part_b, part_g, hidden, feats,
    edge_out, edge_in, turned, outbox, inbox, scale_in, onehot, total, wsum, pick_cols, cols, side_in, col_in, row_in,
    edge_send, edge_recv, send_sem, recv_sem, ssend_sem, srecv_sem, hsend, hrecv, out_sem,
):
    cam = lax.axis_index("cam")
    row = lax.axis_index("row")
    cams = lax.axis_size("cam")
    strips = lax.axis_size("row")
    me = cam * strips + row

    barrier = pltpu.get_barrier_semaphore()

    def greet(i, carry):
        p = lax.rem(me + i, PEERS)
        pl.semaphore_signal(barrier, inc=1, device_id=(p // strips, p % strips), device_id_type=MESH)
        return carry

    lax.fori_loop(1, PEERS, greet, 0)

    repeat = jnp.where(iota((CAP, TL), 1) % CAP == iota((CAP, TL), 0), 1.0, 0.0).astype(BF16)
    def table(numbers):
        return lax.dot_general(numbers.astype(F32).astype(BF16), repeat, TN, preferred_element_type=F32)

    scale_table = table(code_rows[...] >> 16) * 0.0625
    tile_table = table(tile_rows[...] >> 5) * 32.0 + table(tile_rows[...] & 31)
    for i in range(PEERS // 8):
        at = slice(i * 8, i * 8 + 8)
        scale_rows[at] = scale_table[at].reshape(8, 1, TL)
        tiles[at] = tile_table[at].reshape(8, 1, TL)

    def edges(n, carry):
        at = pl.ds(pl.multiple_of(n * 256, 256), 256)
        for half in range(2):
            field = image[:, half * 16 : half * 16 + 16, at].reshape(256, 256)
            first = 14 if half == 1 else 0
            m, k = iota((32, 256), 0), iota((32, 256), 1)
            pick = jnp.where(k == (m % C) * 16 + first + m // C, 1.0, 0.0).astype(BF16)
            edge_out[half, :, at] = dot(pick, field).astype(BF16)
        return carry

    lax.fori_loop(0, W // 256, edges, 0)
    up = (cam, lax.rem(row + strips - 1, strips))
    down = (cam, lax.rem(row + 1, strips))
    for b, taps in enumerate(band(w1[...], 288, 256, row_major(-1), channel_major(0))):
        band1[b] = taps
    for b, taps in enumerate(band(w1[...], 32, 32, row_major(-1), row_major(-2))):
        band1h[0, b] = taps
    for b, taps in enumerate(band(w1[...], 32, 32, row_major(31), row_major(32))):
        band1h[1, b] = taps
    for b, taps in enumerate(band(w2[...], 224, 256, row_major(0), row_major(-1))):
        band2[b] = taps

    def first_main(n, carry):
        at = pl.ds(pl.multiple_of(n * 256, 256), 256)
        for half, part in ((0, part_a), (1, part_b)):
            field = image[:, half * 16 : half * 16 + 16, at].reshape(256, 256)
            for b in range(3):
                part[b, :, at] = dot(band1[b], field)
        return carry

    lax.fori_loop(0, W // 256, first_main, 0)
    pl.semaphore_wait(barrier, PEERS - 1)
    edge_copies = [
        pltpu.make_async_remote_copy(
            src_ref=edge_out.at[half], dst_ref=edge_in.at[half], send_sem=edge_send.at[half], recv_sem=edge_recv.at[half],
            device_id=where, device_id_type=MESH,
        )
        for half, where in ((0, up), (1, down))
    ]
    for copy in edge_copies:
        copy.start()


    def silu(v):
        return v / (1.0 + jnp.exp(-v))

    def hide(at, sources):
        taps = []
        for b in range(3):
            value = None
            for part, first in sources:
                term = part[b, pl.ds(first, 16), :]
                value = term if value is None else value + term
            taps.append(value)
        return silu(shift_add(*taps))

    def put(at, value):
        hidden[pl.ds(at, 16), :] = value.astype(BF16)

    def body_a(i, carry):
        at = pl.multiple_of(i * 16, 16)
        put(at, hide(i, [(part_a, at)]))
        return carry

    def body_b(i, carry):
        at = pl.multiple_of(i * 16, 16)
        put(at, hide(i, [(part_b, pl.multiple_of(at - 256, 16))]))
        return carry

    lax.fori_loop(2, 16, body_a, 0)
    for i in (16, 17):
        put(i * 16, hide(i, [(part_a, i * 16), (part_b, i * 16 - 256)]))
    lax.fori_loop(18, 32, body_b, 0)

    for copy in edge_copies:
        copy.wait()
    has_above = (row > 0).astype(F32)
    has_below = (row < strips - 1).astype(F32)
    above_bf = has_above.astype(BF16)
    below_bf = has_below.astype(BF16)

    def first_edge(n, carry):
        at = pl.ds(pl.multiple_of(n * 256, 256), 256)
        top = edge_in[1, :, at] * above_bf
        bottom = edge_in[0, :, at] * below_bf
        for b in range(3):
            part_g[b, 0:32, at] = dot(band1h[0, b], top)
            part_g[b, 32:64, at] = dot(band1h[1, b], bottom)
        return carry

    lax.fori_loop(0, W // 256, first_edge, 0)
    put(0, hide(0, [(part_a, 0), (part_g, 0)]) * has_above)
    put(16, hide(1, [(part_a, 16), (part_g, 16)]))
    put(512, hide(32, [(part_b, 256), (part_g, 32)]))
    put(528, hide(33, [(part_b, 272), (part_g, 48)]) * has_below)

    def second(n, carry):
        at = pl.ds(pl.multiple_of(n * 256, 256), 256)
        for b in range(3):
            part_a[b, 0:224, at] = dot(band2[b], hidden[0:256, at])
            part_b[b, 0:224, at] = dot(band2[b], hidden[224:480, at])
            part_g[b, :, at] = dot(band2[b, 0:64, 0:96], hidden[448:544, at])
        return carry

    lax.fori_loop(0, W // 256, second, 0)

    def feature_row(part, first):
        def body(i, carry):
            at = pl.ds(pl.multiple_of(i * 16, 16), 16)
            value = shift_add(part[0, at, :], part[1, at, :], part[2, at, :]).astype(BF16).astype(F32)
            for t in range(W // TL):
                feats[(first + i) * (W // TL) + t] = value[:, t * TL : (t + 1) * TL]
            return carry

        return body

    lax.fori_loop(0, 14, feature_row(part_a, 0), 0)
    lax.fori_loop(0, 14, feature_row(part_b, 14), 0)
    lax.fori_loop(0, 4, feature_row(part_g, 28), 0)

    my, mx, mc = cam // 8, lax.rem(cam // 2, 4), lax.rem(cam, 2)

    def offset(t):
        i, c, b = t % 4, (t // 8) % 4, t // 32

        def order(v):
            w = lax.rem(v, 4)
            return lax.rem(2 * w, 3) + 3 * (w // 3)

        return order(i + b), order(i), (t // 4) % 2, order(i + c)

    def moved(core, sign, t):
        dy, dx, _, dz = offset(t)
        place = (lax.rem(my + 4 + sign * dy, 4) * 4 + lax.rem(mx + 4 + sign * dx, 4)) * 2 + core
        return place * 4 + lax.rem(row + 4 + sign * dz, 4)

    def peer_of(t):
        return moved(lax.rem(mc + offset(t)[2], 2), 1 - 2 * mc, t)

    def source_of(t):
        core = lax.rem(mc + offset(t)[2], 2)
        return moved(core, 2 * core - 1, t)

    def make(p, slot, put_tile):
        for e in range(CAP):
            word = code[e, p]
            block = word & 511
            shift = (word >> 9) & 127
            scale = (word >> 16).astype(F32) * 0.0625
            turned[slot, e * C : (e + 1) * C, :] = pltpu.roll(feats[block], shift, 1) * scale
        for q in range(C):
            put_tile(q, turned[slot, pl.ds(q, CAP, stride=C), :].astype(BF16))

    def put_own(q, value):
        inbox[0, q] = value

    make(me, 0, put_own)
    scale_in[0] = scale_rows[me]

    def block_copy(t, p):
        return pltpu.make_async_remote_copy(
            src_ref=outbox.at[t], dst_ref=inbox.at[t], send_sem=send_sem,
            recv_sem=recv_sem.at[t // GROUP], device_id=(p // strips, p % strips), device_id_type=MESH,
        )

    def scale_copy(t, p):
        return pltpu.make_async_remote_copy(
            src_ref=scale_rows.at[p], dst_ref=scale_in.at[t], send_sem=ssend_sem, recv_sem=srecv_sem,
            device_id=(p // strips, p % strips), device_id_type=MESH,
        )

    def send_step(t, carry):
        p = peer_of(t)

        def put_tile(q, value):
            outbox[t, q] = value

        make(p, lax.rem(t, 2), put_tile)

        scale_copy(t, p).start()
        block_copy(t, p).start()
        return carry

    lax.fori_loop(1, PEERS, send_step, 0)

    def pick_body(q, carry):
        j, lane = iota((TL, 256), 0), iota((TL, 256), 1)
        hit = ((j == 0) & (lane == q)) | ((j == TL - 1) & (lane == q + TL))
        pick_cols[pl.ds(pl.multiple_of(q * TL, TL), TL), :] = jnp.where(hit, 1.0, 0.0).astype(BF16)
        return carry

    lax.fori_loop(0, C, pick_body, 0)

    def clear(i, carry):
        total[pl.ds(pl.multiple_of(i * 1024, 1024), 1024), :] = jnp.zeros((1024, TL), F32)
        return carry

    lax.fori_loop(0, C, clear, 0)
    wsum[...] = jnp.zeros_like(wsum)
    col_sum[...] = jnp.zeros_like(col_sum)

    def uv_in(i):
        late = i - 256
        return (
            jnp.where(i < 256, i // 16, late % C),
            jnp.where(i < 256, i % 16, jnp.where(late < C, -1, 16)),
        )

    for b, taps in enumerate(band(wuv[...], 256, 288, channel_major(0), uv_in)):
        band_uv[b * 256 : (b + 1) * 256, :] = taps

    lane = iota((TL, TL), 1)
    sub = iota((TL, TL), 0)
    pick = jnp.where(iota((TL, C), 0) % C == iota((TL, C), 1), 1.0, 0.0).astype(BF16)
    uv_rows = dot(pick, wuv[...]).astype(BF16)
    for side in range(2):
        for a in range(3):
            source = iota((9 * C, TL), 0)
            spread = jnp.where(source == (3 * a + 2 * side) * C + iota((9 * C, TL), 1) % C, 1.0, 0.0).astype(BF16)
            side_mats[side, a] = jnp.where(sub // C == lane // C, dot(uv_rows, spread), 0.0).astype(BF16)

    def wait_group(g, count):
        pltpu.make_async_remote_copy(
            src_ref=outbox.at[pl.ds(0, count)], dst_ref=inbox.at[pl.ds(0, count)], send_sem=send_sem,
            recv_sem=recv_sem.at[g], device_id=up, device_id_type=MESH,
        ).wait_recv()

    def lanes_of(ref, g, half):
        first = g * GROUP + half * 8
        lane = iota((1, TL), 1) // CAP
        value = jnp.zeros((1, TL), ref.dtype)
        for i in range(8):
            index = first + i if ref is scale_in else source_of(first + i)
            value = jnp.where(lane == i, ref[index], value)
        return value

    def mark_group(g):
        ids = jnp.concatenate([lanes_of(tiles, g, 0), lanes_of(tiles, g, 1)], axis=1)
        for m in range(4):
            hot = jnp.where((iota((256, 256), 0) + m * 256).astype(F32) == ids, 1.0, 0.0).astype(BF16)
            onehot[m * 256 : (m + 1) * 256, :] = hot

    def weigh_group(g, carry):
        mark_group(g)
        weights = jnp.concatenate([lanes_of(scale_in, g, 0), lanes_of(scale_in, g, 1)], axis=1)
        weights = jnp.broadcast_to(weights, (TL, 256)).astype(BF16)
        for m in range(4):
            at = slice(m * 256, (m + 1) * 256)
            wsum[at, :] += lax.dot_general(onehot[at, :], weights, NT, preferred_element_type=F32)
        return carry

    def group_sum(g, t, m):
        block = jnp.concatenate(
            [inbox[pl.ds(g * GROUP, GROUP), 2 * t + h].reshape(256, TL) for h in range(2)], axis=1
        )
        return dot(onehot[m * 1024 : (m + 1) * 1024, :], block)

    def add_columns(g):
        rows = [inbox[pl.ds(g * GROUP, GROUP), q].reshape(256, TL) for q in range(C)]
        picked = dot(jnp.concatenate(rows, axis=1), pick_cols[...]).astype(BF16)
        for m in range(4):
            at = slice(m * 256, (m + 1) * 256)
            col_sum[at, :] += dot(onehot[at, :], picked)

    def add_group(g):
        add_columns(g)

        def channels(t, carry):
            for m in range(1):
                got = group_sum(g, t, m)
                for h in range(2):
                    at = pl.ds(pl.multiple_of((2 * t + h) * AR_DEV + m * 1024, 1024), 1024)
                    total[at, :] += got[:, h * TL : (h + 1) * TL]
            return carry

        lax.fori_loop(0, C // 2, channels, 0)

    mark_group(0)
    wait_group(0, GROUP - 1)
    add_group(0)

    def receive(g, carry):
        mark_group(g)
        wait_group(g, GROUP)
        add_group(g)
        return carry

    last = PEERS // GROUP - 1
    lax.fori_loop(1, last, receive, 0)
    pltpu.make_async_remote_copy(
        src_ref=scale_rows.at[pl.ds(0, PEERS - 1)], dst_ref=scale_in.at[pl.ds(0, PEERS - 1)], send_sem=ssend_sem,
        recv_sem=srecv_sem, device_id=up, device_id_type=MESH,
    ).wait()
    lax.fori_loop(0, PEERS // GROUP, weigh_group, 0)
    wsum[...] = 1.0 / jnp.maximum(wsum[...], 1.0)
    wait_group(last, GROUP)

    add_columns(last)

    def collect(rb, carry):
        at = pl.ds(pl.multiple_of(rb * TL, TL), TL)
        values = [(col_sum[at, side * TL : (side + 1) * TL] * wsum[at, :]).astype(BF16).astype(F32) for side in range(2)]
        return tuple(c + pltpu.roll(v, rb * C, 1) for c, v in zip(carry, values))

    zero = jnp.zeros((TL, TL), F32)
    left, right = lax.fori_loop(0, AR_DEV // TL, collect, (zero, zero))
    cols[0] = left.astype(BF16)
    cols[1] = right.astype(BF16)

    west, east = lax.rem(cam + cams - 1, cams), lax.rem(cam + 1, cams)
    north, south = lax.rem(row + strips - 1, strips), lax.rem(row + 1, strips)
    plan = [
        (cols.at[1], side_in.at[0], (east, row)),
        (cols.at[0], side_in.at[1], (west, row)),
        (cols.at[1, pl.ds(112, 16)], col_in.at[0], (east, south)),
        (cols.at[1, pl.ds(0, 16)], col_in.at[1], (east, north)),
        (cols.at[0, pl.ds(112, 16)], col_in.at[2], (west, south)),
        (cols.at[0, pl.ds(0, 16)], col_in.at[3], (west, north)),
        (above.at[64], row_in.at[0], (cam, south)),
        (below.at[0], row_in.at[1], (cam, north)),
    ]
    copies = [
        pltpu.make_async_remote_copy(
            src_ref=src, dst_ref=dst, send_sem=hsend.at[i], recv_sem=hrecv.at[i], device_id=where, device_id_type=MESH
        )
        for i, (src, dst, where) in enumerate(plan)
    ]
    for copy in copies[:6]:
        copy.start()

    def out_copy(t):
        at = pl.ds(2 * t, 2)
        return pltpu.make_async_copy(joined.at[at], joined_out.at[at], out_sem.at[t])

    def finish(t, carry):
        for m in range(1):
            got = group_sum(last, t, m)
            for h in range(2):
                at = pl.ds(pl.multiple_of((2 * t + h) * AR_DEV + m * 1024, 1024), 1024)
                value = (total[at, :] + got[:, h * TL : (h + 1) * TL]) * wsum[m * 1024 : (m + 1) * 1024, :]
                total[at, :] = value
                joined[2 * t + h, m * 1024 : (m + 1) * 1024, :] = value.astype(BF16)
        out_copy(t).start()
        return carry

    lax.fori_loop(0, C // 2, finish, 0)

    def ends(g, carry):
        for last in range(2):
            r = g * 16 + 15 * last
            value = total[pl.ds(r, C, stride=AR_DEV), :].astype(BF16)
            if last:
                above[g + 1] = value
            else:
                below[g] = value
        return carry

    lax.fori_loop(0, 64, ends, 0)

    for copy in copies[6:]:
        copy.start()
    for copy in copies[:6]:
        copy.wait()

    has_side = ((cam > 0).astype(F32), (cam < cams - 1).astype(F32))
    for side in range(2):
        own = side_in[side].astype(F32) * has_side[side]
        top = col_in[2 * side].astype(F32)[15:16, :] * (has_side[side] * has_above)
        bottom = col_in[2 * side + 1].astype(F32)[0:1, :] * (has_side[side] * has_below)
        before = jnp.where(lane[0:1] >= TL - C, top, own[TL - 1 : TL, :])
        before = pltpu.roll(jnp.broadcast_to(before, (TL, TL)), C, 1)
        after = jnp.where(lane[0:1] < C, bottom, own[0:1, :])
        after = pltpu.roll(jnp.broadcast_to(after, (TL, TL)), TL - C, 1)
        shifted = (
            jnp.where(sub == 0, before, pltpu.roll(own, 1, 0)),
            own,
            jnp.where(sub == TL - 1, after, pltpu.roll(own, TL - 1, 0)),
        )
        result = jnp.zeros((TL, TL), F32)
        for a in range(3):
            result = result + lax.dot_general(
                shifted[a].astype(BF16), side_mats[side, a], NT, preferred_element_type=F32
            )
        high = result.astype(BF16)
        side_parts[2 * side] = high
        side_parts[2 * side + 1] = (result - high.astype(F32)).astype(BF16)

    pltpu.make_async_remote_copy(
        src_ref=outbox.at[pl.ds(0, PEERS - 1)], dst_ref=inbox.at[pl.ds(0, PEERS - 1)], send_sem=send_sem,
        recv_sem=recv_sem.at[0], device_id=up, device_id_type=MESH,
    ).wait_send()
    for copy in copies[6:]:
        copy.wait()
    above[0] = row_in[0] * above_bf
    below[64] = row_in[1] * below_bf

    def out_wait(t, carry):
        out_copy(t).wait()
        return carry

    lax.fori_loop(0, C // 2, out_wait, 0)


def uv_kernel(joined, above, below, bands, side_parts, spread_mat, texture, side_plane):
    for half in range(2):
        rb = pl.program_id(0) * 2 + half
        lane = iota((TL, TL), 1)
        parts = jnp.zeros((TL, TL), F32)
        for k in range(4):
            turned = pltpu.roll(side_parts[k].astype(F32), lax.rem(k * C + TL - rb * C, TL), 1)
            parts = jnp.where(lane // C == k, turned, parts)
        parts = parts.astype(BF16)
        for n in range(4):
            at = slice(n * 512, (n + 1) * 512)
            side_plane[:, at] = dot(parts, spread_mat[:, at])
        tile_lane = iota((16, TL), 1)
        for pair in range(4):
            fields = []
            for h in range(2):
                g = pair * 2 + h
                here = slice(half * TL + g * 16, half * TL + (g + 1) * 16)
                fields.append(
                    jnp.concatenate([joined[:, here, :].reshape(256, TL), above[rb * 8 + g], below[rb * 8 + g + 1]], axis=0)
                )
            taps = dot(bands[...], jnp.concatenate(fields, axis=1))
            for h in range(2):
                g = pair * 2 + h
                here = slice(half * TL + g * 16, half * TL + (g + 1) * 16)
                cut = slice(h * TL, (h + 1) * TL)
                a = pltpu.roll(taps[0:256, cut], 1, 1)
                m = taps[256:512, cut]
                b = pltpu.roll(taps[512:768, cut], TL - 1, 1)
                for o in range(C):
                    rows = slice(o * 16, (o + 1) * 16)
                    low = jnp.where(tile_lane == 0, 0.0, a[rows])
                    high = jnp.where(tile_lane == TL - 1, 0.0, b[rows])
                    side = side_plane[g * 16 : (g + 1) * 16, o * TL : (o + 1) * TL]
                    value = joined[o, here, :].astype(F32) + side + m[rows] + low + high
                    texture[o, here, :] = value.astype(BF16)


def local(image, conv_first, conv_second, conv_uv, send_block, send_shift, send_weight, send_count, recv_tile):
    valid = lax.broadcasted_iota(jnp.int32, (CAP, PEERS), 0) < send_count.reshape(1, PEERS)
    weight = jnp.where(valid, send_weight.reshape(PEERS, CAP).T, 0)
    code = send_block.reshape(PEERS, CAP).T + send_shift.reshape(PEERS, CAP).T * 512 + weight * 65536
    tile_rows = recv_tile.reshape(PEERS, CAP).T

    vmem = pl.BlockSpec(memory_space=pltpu.VMEM)
    smem = pl.BlockSpec(memory_space=pltpu.SMEM)
    dma = pltpu.SemaphoreType.DMA
    joined, above, below, bands, side_parts = pl.pallas_call(
        join_kernel,
        out_shape=[
            jax.ShapeDtypeStruct((C, AR_DEV, TL), BF16),
            jax.ShapeDtypeStruct((65, C, TL), BF16),
            jax.ShapeDtypeStruct((65, C, TL), BF16),
            jax.ShapeDtypeStruct((768, 288), BF16),
            jax.ShapeDtypeStruct((4, TL, TL), BF16),
        ],
        in_specs=[vmem, vmem, vmem, vmem, smem, vmem, vmem],
        out_specs=[pl.BlockSpec(memory_space=pl.ANY)] + [vmem] * 4,
        scratch_shapes=[
            pltpu.VMEM((C, AR_DEV, TL), BF16),
            pltpu.VMEM((PEERS, 1, TL), F32),
            pltpu.VMEM((PEERS, 1, TL), F32),
            pltpu.VMEM((2, 3, TL, TL), BF16),
            pltpu.VMEM((AR_DEV, 256), F32),
            pltpu.VMEM((3, 288, 256), BF16),
            pltpu.VMEM((2, 3, 32, 32), BF16),
            pltpu.VMEM((3, 224, 256), BF16),
            pltpu.VMEM((3, 288, W), F32),
            pltpu.VMEM((3, 288, W), F32),
            pltpu.VMEM((3, 64, W), F32),
            pltpu.VMEM((544, W), BF16),
            pltpu.VMEM((512, C, TL), F32),
            pltpu.VMEM((2, 32, W), BF16),
            pltpu.VMEM((2, 32, W), BF16),
            pltpu.VMEM((2, CAP * C, TL), F32),
            pltpu.VMEM((PEERS, C, CAP, TL), BF16),
            pltpu.VMEM((PEERS, C, CAP, TL), BF16),
            pltpu.VMEM((PEERS, 1, TL), F32),
            pltpu.VMEM((AR_DEV, 256), BF16),
            pltpu.VMEM((C * AR_DEV, TL), F32),
            pltpu.VMEM((AR_DEV, TL), F32),
            pltpu.VMEM((C * TL, 256), BF16),
            pltpu.VMEM((2, TL, TL), BF16),
            pltpu.VMEM((2, TL, TL), BF16),
            pltpu.VMEM((4, 16, TL), BF16),
            pltpu.VMEM((2, C, TL), BF16),
            dma((2,)), dma((2,)), dma, dma((PEERS // GROUP,)), dma, dma, dma((8,)), dma((8,)), dma((8,)),
        ],
        compiler_params=pltpu.CompilerParams(
            collective_id=0, has_side_effects=True, vmem_limit_bytes=62 * 1024 * 1024
        ),
        cost_estimate=pl.CostEstimate(flops=2 * 10**10, bytes_accessed=3 * 10**7, transcendentals=10**6),
    )(image.reshape(C, ROWS, W), conv_first, conv_second, conv_uv, code, code, tile_rows)

    k, o = np.arange(TL)[:, None, None] // C, np.arange(TL)[:, None, None] % C
    channel, column = np.arange(C)[None, :, None], np.arange(TL)[None, None, :]
    spread = ((k < 4) & (o == channel) & (column == np.where(k < 2, 0, TL - 1))).reshape(TL, C * TL)
    full = lambda shape: pl.BlockSpec(shape, lambda i: (0,) * len(shape))
    return pl.pallas_call(
        uv_kernel,
        out_shape=jax.ShapeDtypeStruct((C, AR_DEV, TL), BF16),
        grid=(AR_DEV // TL // 2,),
        in_specs=[
            pl.BlockSpec((C, 2 * TL, TL), lambda i: (0, i, 0)),
            full((65, C, TL)),
            full((65, C, TL)),
            full((768, 288)),
            full((4, TL, TL)),
            full((TL, C * TL)),
        ],
        out_specs=pl.BlockSpec((C, 2 * TL, TL), lambda i: (0, i, 0)),
        scratch_shapes=[pltpu.VMEM((TL, C * TL), F32)],
        compiler_params=pltpu.CompilerParams(vmem_limit_bytes=62 * 1024 * 1024),
        cost_estimate=pl.CostEstimate(flops=10**10, bytes_accessed=10**7, transcendentals=0),
    )(joined, above, below, bands, side_parts, jnp.asarray(spread.astype(np.float32)).astype(BF16))


def solution(mesh):
    return jax.shard_map(
        local,
        mesh=mesh,
        in_specs=(
            P("cam", None, "row", None),
            P(),
            P(),
            P(),
            P("cam", "row", None, None),
            P("cam", "row", None, None),
            P("cam", "row", None, None),
            P("cam", "row", None),
            P("row", "cam", None, None),
        ),
        out_specs=P(None, "row", "cam"),
        check_vma=False,
    )
```

```python
import functools

import jax
import jax.numpy as jnp
import numpy as np
from jax import lax
from jax.experimental import pallas as pl
from jax.experimental.pallas import tpu as pltpu
from jax.sharding import PartitionSpec as P

C = 16
W = 2048
TL = 128
CAP = 16
AR_DEV = 1024
PEERS = 128
GROUP = 16
ROWS = 32
F32 = jnp.float32
BF16 = jnp.bfloat16
MESH = pl.DeviceIdType.MESH
NT = (((1,), (1,)), ((), ()))
TN = (((0,), (0,)), ((), ()))


def iota(shape, dim):
    return lax.broadcasted_iota(jnp.int32, shape, dim)


def dot(a, b):
    return jnp.dot(a, b, preferred_element_type=F32)


def band(weight, m, k, out_of_m, in_of_k):
    pick = jnp.where(out_of_m(iota((m, C), 0))[0] == iota((m, C), 1), 1.0, 0.0).astype(BF16)
    rows = dot(pick, weight).astype(BF16)
    step = in_of_k(iota((m, k), 1))[1] - out_of_m(iota((m, k), 0))[1] + 1
    channel = in_of_k(iota((9 * C, k), 1))[0]
    source = iota((9 * C, k), 0)
    taps = []
    for b in range(3):
        total = jnp.zeros((m, k), F32)
        for a in range(3):
            spread = jnp.where(source == (3 * a + b) * C + channel, 1.0, 0.0).astype(BF16)
            total = total + jnp.where(step == a, dot(rows, spread), 0.0)
        taps.append(total.astype(BF16))
    return taps


def row_major(first):
    return lambda i: (i % C, i // C + first)


def channel_major(first):
    return lambda i: (i // 16, i % 16 + first)


def shift_add(left, mid, right):
    n = mid.shape[1]
    lane = iota(mid.shape, 1)
    a = jnp.where(lane == 0, 0.0, pltpu.roll(left, 1, 1))
    b = jnp.where(lane == n - 1, 0.0, pltpu.roll(right, n - 1, 1))
    return mid + a + b


def join_kernel(
    image, w1, w2, wuv, code, code_rows, tile_rows,
    joined_out, above, below, band_uv, side_parts,
    joined, scale_rows, tiles, side_mats, col_sum,
    band1, band1h, band2, part_a, part_b, part_g, hidden, feats,
    edge_out, edge_in, turned, outbox, inbox, scale_in, onehot, total, wsum, pick_cols, cols, side_in, col_in, row_in,
    edge_send, edge_recv, send_sem, recv_sem, ssend_sem, srecv_sem, hsend, hrecv, out_sem,
):
    cam = lax.axis_index("cam")
    row = lax.axis_index("row")
    cams = lax.axis_size("cam")
    strips = lax.axis_size("row")
    me = cam * strips + row

    barrier = pltpu.get_barrier_semaphore()

    def greet(i, carry):
        p = lax.rem(me + i, PEERS)
        pl.semaphore_signal(barrier, inc=1, device_id=(p // strips, p % strips), device_id_type=MESH)
        return carry

    lax.fori_loop(1, PEERS, greet, 0)

    def edges(n, carry):
        at = pl.ds(pl.multiple_of(n * 256, 256), 256)
        for half in range(2):
            field = image[:, half * 16 : half * 16 + 16, at].reshape(256, 256)
            first = 14 if half == 1 else 0
            m, k = iota((32, 256), 0), iota((32, 256), 1)
            pick = jnp.where(k == (m % C) * 16 + first + m // C, 1.0, 0.0).astype(BF16)
            edge_out[half, :, at] = dot(pick, field).astype(BF16)
        return carry

    lax.fori_loop(0, W // 256, edges, 0)
    up = (cam, lax.rem(row + strips - 1, strips))
    down = (cam, lax.rem(row + 1, strips))
    for b, taps in enumerate(band(w1[...], 288, 256, row_major(-1), channel_major(0))):
        band1[b] = taps
    for b, taps in enumerate(band(w1[...], 32, 32, row_major(-1), row_major(-2))):
        band1h[0, b] = taps
    for b, taps in enumerate(band(w1[...], 32, 32, row_major(31), row_major(32))):
        band1h[1, b] = taps
    for b, taps in enumerate(band(w2[...], 224, 256, row_major(0), row_major(-1))):
        band2[b] = taps

    def first_main(n, carry):
        at = pl.ds(pl.multiple_of(n * 256, 256), 256)
        for half, part in ((0, part_a), (1, part_b)):
            field = image[:, half * 16 : half * 16 + 16, at].reshape(256, 256)
            for b in range(3):
                part[b, :, at] = dot(band1[b], field)
        return carry

    lax.fori_loop(0, W // 256, first_main, 0)
    pl.semaphore_wait(barrier, PEERS - 1)
    edge_copies = [
        pltpu.make_async_remote_copy(
            src_ref=edge_out.at[half], dst_ref=edge_in.at[half], send_sem=edge_send.at[half], recv_sem=edge_recv.at[half],
            device_id=where, device_id_type=MESH,
        )
        for half, where in ((0, up), (1, down))
    ]
    for copy in edge_copies:
        copy.start()


    def silu(v):
        return v / (1.0 + jnp.exp(-v))

    def hide(at, sources):
        taps = []
        for b in range(3):
            value = None
            for part, first in sources:
                term = part[b, pl.ds(first, 16), :]
                value = term if value is None else value + term
            taps.append(value)
        return silu(shift_add(*taps))

    def put(at, value):
        hidden[pl.ds(at, 16), :] = value.astype(BF16)

    def body_a(i, carry):
        at = pl.multiple_of(i * 16, 16)
        put(at, hide(i, [(part_a, at)]))
        return carry

    def body_b(i, carry):
        at = pl.multiple_of(i * 16, 16)
        put(at, hide(i, [(part_b, pl.multiple_of(at - 256, 16))]))
        return carry

    lax.fori_loop(2, 16, body_a, 0)
    for i in (16, 17):
        put(i * 16, hide(i, [(part_a, i * 16), (part_b, i * 16 - 256)]))
    lax.fori_loop(18, 32, body_b, 0)

    for copy in edge_copies:
        copy.wait()
    has_above = (row > 0).astype(F32)
    has_below = (row < strips - 1).astype(F32)
    above_bf = has_above.astype(BF16)
    below_bf = has_below.astype(BF16)

    def first_edge(n, carry):
        at = pl.ds(pl.multiple_of(n * 256, 256), 256)
        top = edge_in[1, :, at] * above_bf
        bottom = edge_in[0, :, at] * below_bf
        for b in range(3):
            part_g[b, 0:32, at] = dot(band1h[0, b], top)
            part_g[b, 32:64, at] = dot(band1h[1, b], bottom)
        return carry

    lax.fori_loop(0, W // 256, first_edge, 0)
    put(0, hide(0, [(part_a, 0), (part_g, 0)]) * has_above)
    put(16, hide(1, [(part_a, 16), (part_g, 16)]))
    put(512, hide(32, [(part_b, 256), (part_g, 32)]))
    put(528, hide(33, [(part_b, 272), (part_g, 48)]) * has_below)

    def second(n, carry):
        at = pl.ds(pl.multiple_of(n * 256, 256), 256)
        for b in range(3):
            part_a[b, 0:224, at] = dot(band2[b], hidden[0:256, at])
            part_b[b, 0:224, at] = dot(band2[b], hidden[224:480, at])
            part_g[b, :, at] = dot(band2[b, 0:64, 0:96], hidden[448:544, at])
        return carry

    lax.fori_loop(0, W // 256, second, 0)

    def feature_row(part, first):
        def body(i, carry):
            at = pl.ds(pl.multiple_of(i * 16, 16), 16)
            value = shift_add(part[0, at, :], part[1, at, :], part[2, at, :]).astype(BF16).astype(F32)
            for t in range(W // TL):
                feats[(first + i) * (W // TL) + t] = value[:, t * TL : (t + 1) * TL]
            return carry

        return body

    lax.fori_loop(0, 14, feature_row(part_a, 0), 0)
    lax.fori_loop(0, 14, feature_row(part_b, 14), 0)
    lax.fori_loop(0, 4, feature_row(part_g, 28), 0)

    my, mx, mc = cam // 8, lax.rem(cam // 2, 4), lax.rem(cam, 2)

    def offset(t):
        i, c, b = t % 4, (t // 8) % 4, t // 32

        def order(v):
            w = lax.rem(v, 4)
            return lax.rem(2 * w, 3) + 3 * (w // 3)

        return order(i + b), order(i), (t // 4) % 2, order(i + c)

    def moved(core, sign, t):
        dy, dx, _, dz = offset(t)
        place = (lax.rem(my + 4 + sign * dy, 4) * 4 + lax.rem(mx + 4 + sign * dx, 4)) * 2 + core
        return place * 4 + lax.rem(row + 4 + sign * dz, 4)

    def peer_of(t):
        return moved(lax.rem(mc + offset(t)[2], 2), 1 - 2 * mc, t)

    def source_of(t):
        core = lax.rem(mc + offset(t)[2], 2)
        return moved(core, 2 * core - 1, t)

    def make(p, slot, put_tile):
        for e in range(CAP):
            word = code[e, p]
            block = word & 511
            shift = (word >> 9) & 127
            scale = (word >> 16).astype(F32) * 0.0625
            turned[slot, e * C : (e + 1) * C, :] = pltpu.roll(feats[block], shift, 1) * scale
        for q in range(C):
            put_tile(q, turned[slot, pl.ds(q, CAP, stride=C), :].astype(BF16))

    def put_own(q, value):
        inbox[0, q] = value

    make(me, 0, put_own)

    def block_copy(t, p):
        return pltpu.make_async_remote_copy(
            src_ref=outbox.at[t], dst_ref=inbox.at[t], send_sem=send_sem,
            recv_sem=recv_sem.at[t // GROUP], device_id=(p // strips, p % strips), device_id_type=MESH,
        )

    def scale_copy(t, p):
        return pltpu.make_async_remote_copy(
            src_ref=scale_rows.at[p], dst_ref=scale_in.at[t], send_sem=ssend_sem, recv_sem=srecv_sem,
            device_id=(p // strips, p % strips), device_id_type=MESH,
        )

    def send_step(t, carry):
        p = peer_of(t)

        def put_tile(q, value):
            outbox[t, q] = value

        make(p, lax.rem(t, 2), put_tile)

        block_copy(t, p).start()
        return carry

    lax.fori_loop(1, PEERS, send_step, 0)

    repeat = jnp.where(iota((CAP, TL), 1) % CAP == iota((CAP, TL), 0), 1.0, 0.0).astype(BF16)
    def table(numbers):
        return lax.dot_general(numbers.astype(F32).astype(BF16), repeat, TN, preferred_element_type=F32)

    scale_table = table(code_rows[...] >> 16) * 0.0625
    tile_table = table(tile_rows[...] >> 5) * 32.0 + table(tile_rows[...] & 31)
    for i in range(PEERS // 8):
        at = slice(i * 8, i * 8 + 8)
        scale_rows[at] = scale_table[at].reshape(8, 1, TL)
        tiles[at] = tile_table[at].reshape(8, 1, TL)
    scale_in[0] = scale_rows[me]

    def send_scale(t, carry):
        scale_copy(t, peer_of(t)).start()
        return carry

    lax.fori_loop(1, PEERS, send_scale, 0)

    def pick_body(q, carry):
        j, lane = iota((TL, 256), 0), iota((TL, 256), 1)
        hit = ((j == 0) & (lane == q)) | ((j == TL - 1) & (lane == q + TL))
        pick_cols[pl.ds(pl.multiple_of(q * TL, TL), TL), :] = jnp.where(hit, 1.0, 0.0).astype(BF16)
        return carry

    lax.fori_loop(0, C, pick_body, 0)

    def clear(i, carry):
        total[pl.ds(pl.multiple_of(i * 1024, 1024), 1024), :] = jnp.zeros((1024, TL), F32)
        return carry

    lax.fori_loop(0, C, clear, 0)
    wsum[...] = jnp.zeros_like(wsum)
    col_sum[...] = jnp.zeros_like(col_sum)

    def uv_in(i):
        late = i - 256
        return (
            jnp.where(i < 256, i // 16, late % C),
            jnp.where(i < 256, i % 16, jnp.where(late < C, -1, 16)),
        )

    for b, taps in enumerate(band(wuv[...], 256, 288, channel_major(0), uv_in)):
        band_uv[b * 256 : (b + 1) * 256, :] = taps

    lane = iota((TL, TL), 1)
    sub = iota((TL, TL), 0)
    pick = jnp.where(iota((TL, C), 0) % C == iota((TL, C), 1), 1.0, 0.0).astype(BF16)
    uv_rows = dot(pick, wuv[...]).astype(BF16)
    for side in range(2):
        for a in range(3):
            source = iota((9 * C, TL), 0)
            spread = jnp.where(source == (3 * a + 2 * side) * C + iota((9 * C, TL), 1) % C, 1.0, 0.0).astype(BF16)
            side_mats[side, a] = jnp.where(sub // C == lane // C, dot(uv_rows, spread), 0.0).astype(BF16)

    def wait_group(g, count):
        pltpu.make_async_remote_copy(
            src_ref=outbox.at[pl.ds(0, count)], dst_ref=inbox.at[pl.ds(0, count)], send_sem=send_sem,
            recv_sem=recv_sem.at[g], device_id=up, device_id_type=MESH,
        ).wait_recv()

    def lanes_of(ref, g, half):
        first = g * GROUP + half * 8
        lane = iota((1, TL), 1) // CAP
        value = jnp.zeros((1, TL), ref.dtype)
        for i in range(8):
            index = first + i if ref is scale_in else source_of(first + i)
            value = jnp.where(lane == i, ref[index], value)
        return value

    def mark_group(g):
        ids = jnp.concatenate([lanes_of(tiles, g, 0), lanes_of(tiles, g, 1)], axis=1)
        for m in range(4):
            hot = jnp.where((iota((256, 256), 0) + m * 256).astype(F32) == ids, 1.0, 0.0).astype(BF16)
            onehot[m * 256 : (m + 1) * 256, :] = hot

    def weigh_group(g, carry):
        mark_group(g)
        weights = jnp.concatenate([lanes_of(scale_in, g, 0), lanes_of(scale_in, g, 1)], axis=1)
        weights = jnp.broadcast_to(weights, (TL, 256)).astype(BF16)
        for m in range(4):
            at = slice(m * 256, (m + 1) * 256)
            wsum[at, :] += lax.dot_general(onehot[at, :], weights, NT, preferred_element_type=F32)
        return carry

    def group_sum(g, t, m):
        block = jnp.concatenate(
            [inbox[pl.ds(g * GROUP, GROUP), 2 * t + h].reshape(256, TL) for h in range(2)], axis=1
        )
        return dot(onehot[m * 1024 : (m + 1) * 1024, :], block)

    def add_columns(g):
        rows = [inbox[pl.ds(g * GROUP, GROUP), q].reshape(256, TL) for q in range(C)]
        picked = dot(jnp.concatenate(rows, axis=1), pick_cols[...]).astype(BF16)
        for m in range(4):
            at = slice(m * 256, (m + 1) * 256)
            col_sum[at, :] += dot(onehot[at, :], picked)

    def add_group(g):
        add_columns(g)

        def channels(t, carry):
            for m in range(1):
                got = group_sum(g, t, m)
                for h in range(2):
                    at = pl.ds(pl.multiple_of((2 * t + h) * AR_DEV + m * 1024, 1024), 1024)
                    total[at, :] += got[:, h * TL : (h + 1) * TL]
            return carry

        lax.fori_loop(0, C // 2, channels, 0)

    mark_group(0)
    wait_group(0, GROUP - 1)
    add_group(0)

    def receive(g, carry):
        mark_group(g)
        wait_group(g, GROUP)
        add_group(g)
        return carry

    last = PEERS // GROUP - 1
    lax.fori_loop(1, last, receive, 0)
    pltpu.make_async_remote_copy(
        src_ref=scale_rows.at[pl.ds(0, PEERS - 1)], dst_ref=scale_in.at[pl.ds(0, PEERS - 1)], send_sem=ssend_sem,
        recv_sem=srecv_sem, device_id=up, device_id_type=MESH,
    ).wait()
    lax.fori_loop(0, PEERS // GROUP, weigh_group, 0)
    wsum[...] = 1.0 / jnp.maximum(wsum[...], 1.0)
    wait_group(last, GROUP)

    add_columns(last)

    def collect(rb, carry):
        at = pl.ds(pl.multiple_of(rb * TL, TL), TL)
        values = [(col_sum[at, side * TL : (side + 1) * TL] * wsum[at, :]).astype(BF16).astype(F32) for side in range(2)]
        return tuple(c + pltpu.roll(v, rb * C, 1) for c, v in zip(carry, values))

    zero = jnp.zeros((TL, TL), F32)
    left, right = lax.fori_loop(0, AR_DEV // TL, collect, (zero, zero))
    cols[0] = left.astype(BF16)
    cols[1] = right.astype(BF16)

    west, east = lax.rem(cam + cams - 1, cams), lax.rem(cam + 1, cams)
    north, south = lax.rem(row + strips - 1, strips), lax.rem(row + 1, strips)
    plan = [
        (cols.at[1], side_in.at[0], (east, row)),
        (cols.at[0], side_in.at[1], (west, row)),
        (cols.at[1, pl.ds(112, 16)], col_in.at[0], (east, south)),
        (cols.at[1, pl.ds(0, 16)], col_in.at[1], (east, north)),
        (cols.at[0, pl.ds(112, 16)], col_in.at[2], (west, south)),
        (cols.at[0, pl.ds(0, 16)], col_in.at[3], (west, north)),
        (above.at[64], row_in.at[0], (cam, south)),
        (below.at[0], row_in.at[1], (cam, north)),
    ]
    copies = [
        pltpu.make_async_remote_copy(
            src_ref=src, dst_ref=dst, send_sem=hsend.at[i], recv_sem=hrecv.at[i], device_id=where, device_id_type=MESH
        )
        for i, (src, dst, where) in enumerate(plan)
    ]
    for copy in copies[:6]:
        copy.start()

    def out_copy(t):
        at = pl.ds(2 * t, 2)
        return pltpu.make_async_copy(joined.at[at], joined_out.at[at], out_sem.at[t])

    def finish(t, carry):
        for m in range(1):
            got = group_sum(last, t, m)
            for h in range(2):
                at = pl.ds(pl.multiple_of((2 * t + h) * AR_DEV + m * 1024, 1024), 1024)
                value = (total[at, :] + got[:, h * TL : (h + 1) * TL]) * wsum[m * 1024 : (m + 1) * 1024, :]
                total[at, :] = value
                joined[2 * t + h, m * 1024 : (m + 1) * 1024, :] = value.astype(BF16)
        out_copy(t).start()
        return carry

    lax.fori_loop(0, C // 2, finish, 0)

    def ends(g, carry):
        for last in range(2):
            r = g * 16 + 15 * last
            value = total[pl.ds(r, C, stride=AR_DEV), :].astype(BF16)
            if last:
                above[g + 1] = value
            else:
                below[g] = value
        return carry

    lax.fori_loop(0, 64, ends, 0)

    for copy in copies[6:]:
        copy.start()
    for copy in copies[:6]:
        copy.wait()

    has_side = ((cam > 0).astype(F32), (cam < cams - 1).astype(F32))
    for side in range(2):
        own = side_in[side].astype(F32) * has_side[side]
        top = col_in[2 * side].astype(F32)[15:16, :] * (has_side[side] * has_above)
        bottom = col_in[2 * side + 1].astype(F32)[0:1, :] * (has_side[side] * has_below)
        before = jnp.where(lane[0:1] >= TL - C, top, own[TL - 1 : TL, :])
        before = pltpu.roll(jnp.broadcast_to(before, (TL, TL)), C, 1)
        after = jnp.where(lane[0:1] < C, bottom, own[0:1, :])
        after = pltpu.roll(jnp.broadcast_to(after, (TL, TL)), TL - C, 1)
        shifted = (
            jnp.where(sub == 0, before, pltpu.roll(own, 1, 0)),
            own,
            jnp.where(sub == TL - 1, after, pltpu.roll(own, TL - 1, 0)),
        )
        result = jnp.zeros((TL, TL), F32)
        for a in range(3):
            result = result + lax.dot_general(
                shifted[a].astype(BF16), side_mats[side, a], NT, preferred_element_type=F32
            )
        high = result.astype(BF16)
        side_parts[2 * side] = high
        side_parts[2 * side + 1] = (result - high.astype(F32)).astype(BF16)

    pltpu.make_async_remote_copy(
        src_ref=outbox.at[pl.ds(0, PEERS - 1)], dst_ref=inbox.at[pl.ds(0, PEERS - 1)], send_sem=send_sem,
        recv_sem=recv_sem.at[0], device_id=up, device_id_type=MESH,
    ).wait_send()
    for copy in copies[6:]:
        copy.wait()
    above[0] = row_in[0] * above_bf
    below[64] = row_in[1] * below_bf

    def out_wait(t, carry):
        out_copy(t).wait()
        return carry

    lax.fori_loop(0, C // 2, out_wait, 0)


def uv_kernel(joined, above, below, bands, side_parts, spread_mat, texture, side_plane):
    for half in range(2):
        rb = pl.program_id(0) * 2 + half
        lane = iota((TL, TL), 1)
        parts = jnp.zeros((TL, TL), F32)
        for k in range(4):
            turned = pltpu.roll(side_parts[k].astype(F32), lax.rem(k * C + TL - rb * C, TL), 1)
            parts = jnp.where(lane // C == k, turned, parts)
        parts = parts.astype(BF16)
        for n in range(4):
            at = slice(n * 512, (n + 1) * 512)
            side_plane[:, at] = dot(parts, spread_mat[:, at])
        tile_lane = iota((16, TL), 1)
        for pair in range(4):
            fields = []
            for h in range(2):
                g = pair * 2 + h
                here = slice(half * TL + g * 16, half * TL + (g + 1) * 16)
                fields.append(
                    jnp.concatenate([joined[:, here, :].reshape(256, TL), above[rb * 8 + g], below[rb * 8 + g + 1]], axis=0)
                )
            taps = dot(bands[...], jnp.concatenate(fields, axis=1))
            for h in range(2):
                g = pair * 2 + h
                here = slice(half * TL + g * 16, half * TL + (g + 1) * 16)
                cut = slice(h * TL, (h + 1) * TL)
                a = pltpu.roll(taps[0:256, cut], 1, 1)
                m = taps[256:512, cut]
                b = pltpu.roll(taps[512:768, cut], TL - 1, 1)
                for o in range(C):
                    rows = slice(o * 16, (o + 1) * 16)
                    low = jnp.where(tile_lane == 0, 0.0, a[rows])
                    high = jnp.where(tile_lane == TL - 1, 0.0, b[rows])
                    side = side_plane[g * 16 : (g + 1) * 16, o * TL : (o + 1) * TL]
                    value = joined[o, here, :].astype(F32) + side + m[rows] + low + high
                    texture[o, here, :] = value.astype(BF16)


def local(image, conv_first, conv_second, conv_uv, send_block, send_shift, send_weight, send_count, recv_tile):
    valid = lax.broadcasted_iota(jnp.int32, (CAP, PEERS), 0) < send_count.reshape(1, PEERS)
    weight = jnp.where(valid, send_weight.reshape(PEERS, CAP).T, 0)
    code = send_block.reshape(PEERS, CAP).T + send_shift.reshape(PEERS, CAP).T * 512 + weight * 65536
    tile_rows = recv_tile.reshape(PEERS, CAP).T

    vmem = pl.BlockSpec(memory_space=pltpu.VMEM)
    smem = pl.BlockSpec(memory_space=pltpu.SMEM)
    dma = pltpu.SemaphoreType.DMA
    joined, above, below, bands, side_parts = pl.pallas_call(
        join_kernel,
        out_shape=[
            jax.ShapeDtypeStruct((C, AR_DEV, TL), BF16),
            jax.ShapeDtypeStruct((65, C, TL), BF16),
            jax.ShapeDtypeStruct((65, C, TL), BF16),
            jax.ShapeDtypeStruct((768, 288), BF16),
            jax.ShapeDtypeStruct((4, TL, TL), BF16),
        ],
        in_specs=[vmem, vmem, vmem, vmem, smem, vmem, vmem],
        out_specs=[pl.BlockSpec(memory_space=pl.ANY)] + [vmem] * 4,
        scratch_shapes=[
            pltpu.VMEM((C, AR_DEV, TL), BF16),
            pltpu.VMEM((PEERS, 1, TL), F32),
            pltpu.VMEM((PEERS, 1, TL), F32),
            pltpu.VMEM((2, 3, TL, TL), BF16),
            pltpu.VMEM((AR_DEV, 256), F32),
            pltpu.VMEM((3, 288, 256), BF16),
            pltpu.VMEM((2, 3, 32, 32), BF16),
            pltpu.VMEM((3, 224, 256), BF16),
            pltpu.VMEM((3, 288, W), F32),
            pltpu.VMEM((3, 288, W), F32),
            pltpu.VMEM((3, 64, W), F32),
            pltpu.VMEM((544, W), BF16),
            pltpu.VMEM((512, C, TL), F32),
            pltpu.VMEM((2, 32, W), BF16),
            pltpu.VMEM((2, 32, W), BF16),
            pltpu.VMEM((2, CAP * C, TL), F32),
            pltpu.VMEM((PEERS, C, CAP, TL), BF16),
            pltpu.VMEM((PEERS, C, CAP, TL), BF16),
            pltpu.VMEM((PEERS, 1, TL), F32),
            pltpu.VMEM((AR_DEV, 256), BF16),
            pltpu.VMEM((C * AR_DEV, TL), F32),
            pltpu.VMEM((AR_DEV, TL), F32),
            pltpu.VMEM((C * TL, 256), BF16),
            pltpu.VMEM((2, TL, TL), BF16),
            pltpu.VMEM((2, TL, TL), BF16),
            pltpu.VMEM((4, 16, TL), BF16),
            pltpu.VMEM((2, C, TL), BF16),
            dma((2,)), dma((2,)), dma, dma((PEERS // GROUP,)), dma, dma, dma((8,)), dma((8,)), dma((8,)),
        ],
        compiler_params=pltpu.CompilerParams(
            collective_id=0, has_side_effects=True, vmem_limit_bytes=62 * 1024 * 1024
        ),
        cost_estimate=pl.CostEstimate(flops=2 * 10**10, bytes_accessed=3 * 10**7, transcendentals=10**6),
    )(image.reshape(C, ROWS, W), conv_first, conv_second, conv_uv, code, code, tile_rows)

    k, o = np.arange(TL)[:, None, None] // C, np.arange(TL)[:, None, None] % C
    channel, column = np.arange(C)[None, :, None], np.arange(TL)[None, None, :]
    spread = ((k < 4) & (o == channel) & (column == np.where(k < 2, 0, TL - 1))).reshape(TL, C * TL)
    full = lambda shape: pl.BlockSpec(shape, lambda i: (0,) * len(shape))
    return pl.pallas_call(
        uv_kernel,
        out_shape=jax.ShapeDtypeStruct((C, AR_DEV, TL), BF16),
        grid=(AR_DEV // TL // 2,),
        in_specs=[
            pl.BlockSpec((C, 2 * TL, TL), lambda i: (0, i, 0)),
            full((65, C, TL)),
            full((65, C, TL)),
            full((768, 288)),
            full((4, TL, TL)),
            full((TL, C * TL)),
        ],
        out_specs=pl.BlockSpec((C, 2 * TL, TL), lambda i: (0, i, 0)),
        scratch_shapes=[pltpu.VMEM((TL, C * TL), F32)],
        compiler_params=pltpu.CompilerParams(vmem_limit_bytes=62 * 1024 * 1024),
        cost_estimate=pl.CostEstimate(flops=10**10, bytes_accessed=10**7, transcendentals=0),
    )(joined, above, below, bands, side_parts, jnp.asarray(spread.astype(np.float32)).astype(BF16))


def solution(mesh):
    return jax.shard_map(
        local,
        mesh=mesh,
        in_specs=(
            P("cam", None, "row", None),
            P(),
            P(),
            P(),
            P("cam", "row", None, None),
            P("cam", "row", None, None),
            P("cam", "row", None, None),
            P("cam", "row", None),
            P("row", "cam", None, None),
        ),
        out_specs=P(None, "row", "cam"),
        check_vma=False,
    )
```
